32 devices in a mesh: lat: 8 (over z, y), lon: 4 (over x, core).
Axes of the slice: x: 2, y: 2, z: 4, core: 2. Of those that a mesh axis runs over, the one named last changes fastest.
Arguments:
- grid_state: bfloat16 [1, 32, 1024, 1024], P(None, 'lat', 'lon'), may hold values from -45 to 45
- stencil_one: float32 [2, 3, 1024], replicated, may hold values from -1.5 to 1.5
- stencil_two: float32 [2, 3, 1024], replicated, may hold values from -1.5 to 1.5
- norm_gain: float32 [1024], replicated, may hold values from 0.5 to 1.5
- query_weight: bfloat16 [1024, 1024], replicated, may hold values from -0.125 to 0.125
- key_value_weight: bfloat16 [1024, 512], replicated, may hold values from -3.125 to 3.125
Outputs:
- mixed_field: bfloat16 [1, 32, 1024, 1024], P(None, 'lat', 'lon')
- attended: bfloat16 [1, 32, 1024, 1024], P(None, 'lat', 'lon')
The draws below stay inside these ranges and needn't reach their ends.
All inputs are finite; a program needn't handle non-finite values.
Results may differ from the reference program's by a relative error of at most 0.035.
Values may be sent and summed in bfloat16 or wider, within the bound.
A program may use at most 128 MiB of HBM per device.

```python
import math
import jax
import jax.numpy as jnp
from jax import lax

D = 1024
HEADS = 16
KV_HEADS = 4
HEAD_DIM = 64
LEVELS = 1
NLON = 1024
NLAT = 32


def draw_grid_state(key, part):
    key = jax.random.fold_in(key, 11)
    base_key, row_key, column_key = jax.random.split(key, 3)
    base = jnp.clip(jax.random.normal(base_key, (LEVELS, NLAT, NLON, D), jnp.float32), -4.0, 4.0)
    row_scale = jnp.exp(jax.random.uniform(row_key, (LEVELS, NLAT, NLON, 1), jnp.float32, -1.15, 1.15))
    column_scale = jnp.exp(jax.random.uniform(column_key, (1, 1, 1, D), jnp.float32, -1.15, 1.15))
    return (base * row_scale * column_scale).astype(jnp.bfloat16)


def draw_query_weight(key, part):
    key = jax.random.fold_in(key, 12)
    own = jnp.clip(jax.random.normal(key, (D, HEADS * HEAD_DIM), jnp.float32), -4.0, 4.0) / math.sqrt(D)
    return own.astype(jnp.bfloat16)


def draw_key_value_weight(key, part):
    key = jax.random.fold_in(key, 13)
    key_width = KV_HEADS * HEAD_DIM
    own = jnp.clip(jax.random.normal(key, (D, 2 * key_width), jnp.float32), -4.0, 4.0) / math.sqrt(D)
    return own.astype(jnp.bfloat16)


def gaussian(rng, shape, width, reach, kind=jnp.bfloat16):
    return jnp.clip(width * jax.random.normal(rng, shape, jnp.float32), -reach, reach).astype(kind)


def setup_inputs(seed: int = 0) -> dict:
    arg_keys = jax.random.split(jax.random.key(seed), 7)
    return {
        "grid_state": draw_grid_state(jax.random.fold_in(arg_keys[6], 71), 0),
        "stencil_one": gaussian(arg_keys[1], (2, 3, D), 0.3, 1.5, jnp.float32),
        "stencil_two": gaussian(arg_keys[2], (2, 3, D), 0.3, 1.5, jnp.float32),
        "norm_gain": jnp.clip(1.0 + 0.1 * jax.random.normal(arg_keys[3], (D,), jnp.float32), 0.5, 1.5),
        "query_weight": draw_query_weight(jax.random.fold_in(arg_keys[6], 71), 0),
        "key_value_weight": draw_key_value_weight(jax.random.fold_in(arg_keys[6], 71), 0),
    }


def band_weights(first_row, row_count, nlat_total):
    positions = (jnp.arange(row_count, dtype=jnp.int32) + first_row).astype(jnp.float32)
    return jnp.abs(jnp.sin(jnp.pi * (positions + 0.5) / nlat_total))

def apply_stencil(extended, weights, row_weights):
    scaled = extended.astype(jnp.float32) * row_weights[None, :, None, None]
    column_count = extended.shape[2] - 2
    running = jnp.zeros_like(scaled[:, 1:-1, 1:-1])
    for offset in range(3):
        centre = scaled[:, 1:-1, offset:offset + column_count]
        beside = scaled[:, :-2, offset:offset + column_count] + scaled[:, 2:, offset:offset + column_count]
        running = running + weights[0, offset] * centre + weights[1, offset] * beside
    return (extended[:, 1:-1, 1:-1].astype(jnp.float32) + running).astype(jnp.bfloat16)

def extend_whole(layer_input):
    half_circle = layer_input.shape[2] // 2
    upper_rim = jnp.roll(layer_input[:, :1], -half_circle, axis=2)
    lower_rim = jnp.roll(layer_input[:, -1:], -half_circle, axis=2)
    band_rows = jnp.concatenate([upper_rim, layer_input, lower_rim], axis=1)
    return jnp.concatenate([band_rows[:, :, -1:], band_rows, band_rows[:, :, :1]], axis=2)

def circle_rows(packed):
    query_row, key_row, value_row = packed
    groups = HEADS // KV_HEADS
    queries = query_row.reshape(NLON, HEADS, HEAD_DIM).astype(jnp.float32)
    keys_full = jnp.repeat(key_row.reshape(NLON, KV_HEADS, HEAD_DIM), groups, axis=1).astype(jnp.float32)
    values_full = jnp.repeat(value_row.reshape(NLON, KV_HEADS, HEAD_DIM), groups, axis=1).astype(jnp.float32)
    scores = jnp.einsum('qhd,khd->hqk', queries, keys_full) / math.sqrt(HEAD_DIM)
    row_peak = lax.optimization_barrier(jnp.max(scores, axis=-1, keepdims=True))
    exponent = jnp.exp(scores - row_peak)
    denominator = lax.optimization_barrier(jnp.sum(exponent, axis=-1))
    probs = exponent.astype(jnp.bfloat16).astype(jnp.float32)
    mixed = jnp.einsum('hqk,khd->qhd', probs, values_full) / jnp.transpose(denominator)[:, :, None]
    return mixed.reshape(NLON, HEADS * HEAD_DIM).astype(jnp.bfloat16)

def reference(grid_state, stencil_one, stencil_two, norm_gain, query_weight, key_value_weight):
    row_weights = band_weights(-1, NLAT + 2, NLAT)
    after_one = apply_stencil(extend_whole(grid_state), stencil_one, row_weights)
    mixed_field = apply_stencil(extend_whole(after_one), stencil_two, row_weights)
    flattened = mixed_field.reshape(LEVELS * NLAT * NLON, D).astype(jnp.float32)
    mean_square = lax.optimization_barrier(jnp.mean(flattened * flattened, axis=-1, keepdims=True))
    normed = (flattened * lax.rsqrt(mean_square + 1e-06) * norm_gain).astype(jnp.bfloat16)
    queries = jnp.dot(normed, query_weight, preferred_element_type=jnp.float32).astype(jnp.bfloat16)
    key_values = jnp.dot(normed, key_value_weight, preferred_element_type=jnp.float32).astype(jnp.bfloat16)
    queries = queries.reshape(LEVELS * NLAT, NLON, D)
    key_values = key_values.reshape(LEVELS * NLAT, NLON, 2 * KV_HEADS * HEAD_DIM)
    key_width = KV_HEADS * HEAD_DIM
    attended = lax.map(circle_rows, (queries, key_values[..., :key_width], key_values[..., key_width:]))
    return (mixed_field, attended.reshape(LEVELS, NLAT, NLON, D))
```

```python
import functools
import math

import jax
import jax.numpy as jnp
from jax import lax
from jax.experimental import pallas as pl
from jax.experimental.pallas import tpu as pltpu
from jax.sharding import PartitionSpec as P

HEADS = 16
KV_HEADS = 4
HEAD_DIM = 64
GROUPS = HEADS // KV_HEADS
BLOCK = KV_HEADS * HEAD_DIM
QUERY_SCALE = math.log2(math.e) / math.sqrt(HEAD_DIM)


def lane_group(shape):
    return lax.broadcasted_iota(jnp.int32, shape, len(shape) - 1) // HEAD_DIM


def place_queries(normed, query_weight_ref, placed_ref):
    for g in range(KV_HEADS):
        weight = query_weight_ref[:, g * BLOCK : (g + 1) * BLOCK]
        block = jnp.dot(normed, weight, preferred_element_type=jnp.float32) * QUERY_SCALE
        group = lane_group(block.shape)
        for j in range(GROUPS):
            shift = (g - j) * HEAD_DIM % BLOCK
            moved = pltpu.roll(block, shift, 1) if shift else block
            placed_ref[j, g] = jnp.where(group == g, moved, 0.0).astype(jnp.bfloat16)


def attend(placed_ref, keys, values, mixed_ref, store):
    def one_block(j, carry):
        mixed = jnp.zeros(mixed_ref.shape[1:], jnp.float32)
        group = lane_group(mixed.shape)
        for g in range(KV_HEADS):
            scores = lax.dot_general(
                placed_ref[j, g],
                keys(),
                (((1,), (1,)), ((), ())),
                preferred_element_type=jnp.float32,
            )
            peak = jnp.max(scores, axis=-1, keepdims=True)
            probs = jnp.exp2(scores - peak)
            denominator = jnp.sum(probs, axis=-1, keepdims=True)
            update = jnp.dot(
                probs.astype(jnp.bfloat16), values(), preferred_element_type=jnp.float32
            )
            mixed = jnp.where(group == g, update / denominator, mixed)
        mixed_ref[j] = mixed
        return carry

    lax.fori_loop(0, GROUPS, one_block, 0)
    for g in range(KV_HEADS):
        out = jnp.zeros(mixed_ref.shape[1:], jnp.float32)
        group = lane_group(out.shape)
        for j in range(GROUPS):
            shift = (j - g) * HEAD_DIM % BLOCK
            part = mixed_ref[j]
            moved = pltpu.roll(part, shift, 1) if shift else part
            out = jnp.where(group == j, moved, out)
        store(g, out.astype(jnp.bfloat16))


def attention_kernel(normed_ref, key_value_ref, query_weight_ref, out_ref, placed_ref, mixed_ref):
    place_queries(normed_ref[0], query_weight_ref, placed_ref)

    def store(g, value):
        out_ref[0, :, g * BLOCK : (g + 1) * BLOCK] = value

    attend(
        placed_ref,
        lambda: key_value_ref[0, :, :BLOCK],
        lambda: key_value_ref[0, :, BLOCK:],
        mixed_ref,
        store,
    )


def attention(normed, key_values, query_weight):
    circles, lon_count, channels = normed.shape
    columns = key_values.shape[1]
    return pl.pallas_call(
        attention_kernel,
        grid=(circles,),
        out_shape=jax.ShapeDtypeStruct(normed.shape, jnp.bfloat16),
        in_specs=[
            pl.BlockSpec((1, lon_count, channels), lambda i: (i, 0, 0)),
            pl.BlockSpec((1, columns, 2 * BLOCK), lambda i: (i, 0, 0)),
            pl.BlockSpec((channels, channels), lambda i: (0, 0)),
        ],
        out_specs=pl.BlockSpec((1, lon_count, channels), lambda i: (i, 0, 0)),
        scratch_shapes=[
            pltpu.VMEM((GROUPS, KV_HEADS, lon_count, BLOCK), jnp.bfloat16),
            pltpu.VMEM((GROUPS, lon_count, BLOCK), jnp.float32),
        ],
        compiler_params=pltpu.CompilerParams(vmem_limit_bytes=40 * 1024 * 1024),
    )(normed, key_values, query_weight)


def extended_2(cells, sides, width, closed):
    for axis, dim in sides:
        count = lax.axis_size(axis)
        ends = count if closed else count - 1
        head = lax.slice_in_dim(cells, 0, width, axis=dim)
        tail = lax.slice_in_dim(cells, cells.shape[dim] - width, cells.shape[dim], axis=dim)
        cells = jnp.concatenate(
            [
                lax.ppermute(tail, axis, [(i, (i + 1) % count) for i in range(ends)]),
                cells,
                lax.ppermute(head, axis, [((i + 1) % count, i) for i in range(ends)]),
            ],
            axis=dim,
        )
    return cells


def from_partner(x, axis, distance):
    return lax.ppermute(x, axis, [(i, i ^ 1 << distance) for i in range(lax.axis_size(axis))])


def band_weights(first_row, row_count, nlat_total):
    positions = (jnp.arange(row_count, dtype=jnp.int32) + first_row).astype(jnp.float32)
    return jnp.abs(jnp.sin(jnp.pi * (positions + 0.5) / nlat_total))


def apply_stencil(extended, weights, row_weights):
    scaled = extended.astype(jnp.float32) * row_weights[None, :, None, None]
    column_count = extended.shape[2] - 2
    running = jnp.zeros_like(scaled[:, 1:-1, 1:-1])
    for offset in range(3):
        centre = scaled[:, 1:-1, offset : offset + column_count]
        beside = (
            scaled[:, :-2, offset : offset + column_count]
            + scaled[:, 2:, offset : offset + column_count]
        )
        running = running + weights[0, offset] * centre + weights[1, offset] * beside
    return (extended[:, 1:-1, 1:-1].astype(jnp.float32) + running).astype(jnp.bfloat16)


def place_poles(band_rows, mirrored, margin):
    band_index = lax.axis_index("lat")
    last_band = lax.axis_size("lat") - 1
    upper_rim = jnp.where(band_index == 0, mirrored[:, :margin][:, ::-1], band_rows[:, :margin])
    lower_rim = jnp.where(
        band_index == last_band, mirrored[:, margin:][:, ::-1], band_rows[:, -margin:]
    )
    return jnp.concatenate([upper_rim, band_rows[:, margin:-margin], lower_rim], axis=1)


def extend_once(layer_input):
    band_rows = extended_2(layer_input, (("lat", 1),), 1, False)
    polar_rows = jnp.concatenate([layer_input[:, :1], layer_input[:, -1:]], axis=1)
    mirrored = from_partner(polar_rows, "lon", lax.axis_size("lon").bit_length() - 2)
    band_rows = place_poles(band_rows, mirrored, 1)
    return extended_2(band_rows, (("lon", 2),), 1, True)


def local(grid_state, stencil_one, stencil_two, norm_gain, query_weight, key_value_weight):
    level_count, band_count, lon_count, channels = grid_state.shape
    circles = level_count * band_count
    nlat_total = band_count * lax.axis_size("lat")
    band_start = lax.axis_index("lat") * band_count
    row_weights = band_weights(band_start - 1, band_count + 2, nlat_total)
    after_one = apply_stencil(extend_once(grid_state), stencil_one, row_weights)
    mixed_field = apply_stencil(extend_once(after_one), stencil_two, row_weights)
    flattened = mixed_field.reshape(circles * lon_count, channels).astype(jnp.float32)
    mean_square = jnp.mean(flattened * flattened, axis=-1, keepdims=True)
    normed = (flattened * lax.rsqrt(mean_square + 1e-06) * norm_gain).astype(jnp.bfloat16)
    key_values = jnp.dot(normed, key_value_weight, preferred_element_type=jnp.float32).astype(
        jnp.bfloat16
    )
    key_values = key_values.reshape(circles, lon_count, 2 * BLOCK)
    key_values = lax.all_gather(key_values, "lon", axis=1, tiled=True)
    attended = attention(normed.reshape(circles, lon_count, channels), key_values, query_weight)
    return (mixed_field, attended.reshape(level_count, band_count, lon_count, channels))


def solution(mesh):
    in_specs = (P(None, "lat", "lon", None), P(), P(), P(), P(), P())
    out_specs = (P(None, "lat", "lon", None), P(None, "lat", "lon", None))
    return jax.shard_map(local, mesh=mesh, in_specs=in_specs, out_specs=out_specs, check_vma=False)
```

```python
import functools
import math

import jax
import jax.numpy as jnp
from jax import lax
from jax.experimental import pallas as pl
from jax.experimental.pallas import tpu as pltpu
from jax.sharding import PartitionSpec as P

HEADS = 16
KV_HEADS = 4
HEAD_DIM = 64
GROUPS = HEADS // KV_HEADS
BLOCK = KV_HEADS * HEAD_DIM
EDGE = 16
MESH = pl.DeviceIdType.MESH
QUERY_SCALE = math.log2(math.e) / math.sqrt(HEAD_DIM)


def lane_group(shape):
    return lax.broadcasted_iota(jnp.int32, shape, len(shape) - 1) // HEAD_DIM


def place_queries(normed, query_weight_ref, placed_ref):
    for g in range(KV_HEADS):
        weight = query_weight_ref[:, g * BLOCK : (g + 1) * BLOCK]
        block = jnp.dot(normed, weight, preferred_element_type=jnp.float32) * QUERY_SCALE
        group = lane_group(block.shape)
        for j in range(GROUPS):
            shift = (g - j) * HEAD_DIM % BLOCK
            moved = pltpu.roll(block, shift, 1) if shift else block
            placed_ref[j, g] = jnp.where(group == g, moved, 0.0).astype(jnp.bfloat16)


def attend(placed_ref, keys, values, mixed_ref, store):
    def one_block(j, carry):
        mixed = jnp.zeros(mixed_ref.shape[1:], jnp.float32)
        group = lane_group(mixed.shape)
        for g in range(KV_HEADS):
            scores = lax.dot_general(
                placed_ref[j, g],
                keys(),
                (((1,), (1,)), ((), ())),
                preferred_element_type=jnp.float32,
            )
            peak = jnp.max(scores, axis=-1, keepdims=True)
            probs = jnp.exp2(scores - peak)
            denominator = jnp.sum(probs, axis=-1, keepdims=True)
            update = jnp.dot(
                probs.astype(jnp.bfloat16), values(), preferred_element_type=jnp.float32
            )
            mixed = jnp.where(group == g, update / denominator, mixed)
        mixed_ref[j] = mixed
        return carry

    lax.fori_loop(0, GROUPS, one_block, 0)
    for g in range(KV_HEADS):
        out = jnp.zeros(mixed_ref.shape[1:], jnp.float32)
        group = lane_group(out.shape)
        for j in range(GROUPS):
            shift = (j - g) * HEAD_DIM % BLOCK
            part = mixed_ref[j]
            moved = pltpu.roll(part, shift, 1) if shift else part
            out = jnp.where(group == j, moved, out)
        store(g, out.astype(jnp.bfloat16))

def row_weights(first_row, row_count, nlat_total):
    positions = (jnp.arange(row_count, dtype=jnp.int32) + first_row).astype(jnp.float32)
    return jnp.abs(jnp.sin(jnp.pi * (positions + 0.5) / nlat_total))


def block_kernel(
    lat_size,
    lon_size,
    circle_ref,
    grid_ref,
    stencil_one_ref,
    stencil_two_ref,
    gain_ref,
    query_hbm,
    key_value_hbm,
    mixed_out,
    attended_out,
    wide,
    after_one,
    mixed_field,
    normed,
    key_values,
    placed,
    mixed,
    attended,
    query_weight,
    key_value_weight,
    local_sem,
    out_sem,
    halo_send,
    halo_recv,
    side_send,
    side_recv,
    edge_send,
    edge_recv,
    kv_send,
    kv_recv,
):
    band, width, channels = grid_ref.shape
    last = band - 1
    lat = lax.axis_index("lat")
    lon = lax.axis_index("lon")
    chips = lon_size // 2
    left, right = lax.rem(lon + lon_size - 1, lon_size), lax.rem(lon + 1, lon_size)
    sibling = lon + 1 - 2 * lax.rem(lon, 2)
    partner = lax.rem(lon + lon_size // 2, lon_size)
    at_top, at_bottom = lat == 0, lat == lat_size - 1
    top = (jnp.where(at_top, lat, lat - 1), jnp.where(at_top, partner, lon))
    bottom = (jnp.where(at_bottom, lat, lat + 1), jnp.where(at_bottom, partner, lon))

    def remote(src, dst, send, recv, device):
        return pltpu.make_async_remote_copy(
            src_ref=src,
            dst_ref=dst,
            send_sem=send,
            recv_sem=recv,
            device_id=device,
            device_id_type=MESH,
        )

    loads = [
        pltpu.make_async_copy(
            grid_ref, wide.at[pl.ds(2, band), pl.ds(EDGE, width)], local_sem.at[0]
        ),
        pltpu.make_async_copy(key_value_hbm, key_value_weight, local_sem.at[1]),
        pltpu.make_async_copy(query_hbm, query_weight, local_sem.at[2]),
    ]
    for load in loads:
        load.start()

    barrier = pltpu.get_barrier_semaphore()
    for device in (top, bottom):
        pl.semaphore_signal(barrier, inc=1, device_id=device, device_id_type=MESH)
    for step in range(1, lon_size):
        other = (lat, lax.rem(lon + step, lon_size))
        pl.semaphore_signal(barrier, inc=1, device_id=other, device_id_type=MESH)
    pl.semaphore_wait(barrier, lon_size + 1)

    def halo(row, target, device, slot):
        return remote(
            grid_ref.at[row],
            wide.at[target, pl.ds(EDGE, width)],
            halo_send.at[slot],
            halo_recv.at[target],
            device,
        )

    near_top = halo(0, jnp.where(at_top, 1, band + 2), top, 0)
    near_bottom = halo(last, jnp.where(at_bottom, band + 2, 1), bottom, 1)
    far_top = halo(1, jnp.where(at_top, 0, band + 3), top, 2)
    far_bottom = halo(last - 1, jnp.where(at_bottom, band + 3, 0), bottom, 3)
    sides = [
        remote(
            grid_ref.at[:, pl.ds(width - EDGE, EDGE)],
            wide.at[pl.ds(2, band), pl.ds(0, EDGE)],
            side_send.at[0],
            side_recv.at[0],
            (lat, right),
        ),
        remote(
            grid_ref.at[:, pl.ds(0, EDGE)],
            wide.at[pl.ds(2, band), pl.ds(EDGE + width, EDGE)],
            side_send.at[1],
            side_recv.at[1],
            (lat, left),
        ),
    ]
    near_top.start()
    near_bottom.start()
    for side in sides:
        side.start()
    near_top.wait_send()
    far_top.start()
    near_bottom.wait_send()
    far_bottom.start()

    def edges(row):
        slot = {0: 0, 1: 1, band + 2: 2, band + 3: 3}[row]
        return [
            remote(
                wide.at[row, pl.ds(width, EDGE)],
                wide.at[row, pl.ds(0, EDGE)],
                edge_send.at[slot, 0],
                edge_recv.at[slot, 0],
                (lat, right),
            ),
            remote(
                wide.at[row, pl.ds(EDGE, EDGE)],
                wide.at[row, pl.ds(EDGE + width, EDGE)],
                edge_send.at[slot, 1],
                edge_recv.at[slot, 1],
                (lat, left),
            ),
        ]

    def receive_halos(rows):
        for row in rows:
            halo(0, row, top, 0).wait_recv()
            for edge in edges(row):
                edge.start()
        for row in rows:
            for edge in edges(row):
                edge.wait_recv()

    def stencil(source, first, step, count, circle_first, weights_ref, store):
        total = width + 2 * EDGE
        chunks = channels // 128

        def one(index, carry):
            row = first + index // chunks * step
            circle = circle_first + index // chunks * step
            lanes = pl.ds(pl.multiple_of(index % chunks * 128, 128), 128)
            above = source[row - 1, :, lanes].astype(jnp.float32)
            centre = source[row, :, lanes].astype(jnp.float32)
            below = source[row + 1, :, lanes].astype(jnp.float32)
            beside = circle_ref[circle - 1] * above + circle_ref[circle + 1] * below
            own = weights_ref[0, :, lanes] * circle_ref[circle]
            next_to = weights_ref[1, :, lanes]
            result = centre + own[1:2] * centre + next_to[1:2] * beside
            result = result + pltpu.roll(own[0:1] * centre + next_to[0:1] * beside, 1, 0)
            result = result + pltpu.roll(own[2:3] * centre + next_to[2:3] * beside, total - 1, 0)
            store(row, lanes, result.astype(jnp.bfloat16))
            return carry

        lax.fori_loop(0, count * chunks, one, 0)

    def store_after_one(row, lanes, value):
        after_one[row - 1, :, lanes] = value

    def store_mixed(row, lanes, value):
        mixed_field[row - 1, :, lanes] = value[EDGE : EDGE + width]

    def own_columns(owner):
        return pl.ds(pl.multiple_of(owner * width, EDGE), width)

    def kv_copy(row, owner, device, slot):
        block = key_values.at[row, own_columns(owner)]
        return remote(block, block, kv_send.at[row, slot], kv_recv.at[row, owner], device)

    def kv_start(row):
        for step in range(1, chips):
            other = lax.rem(lon + 2 * step, lon_size)
            kv_copy(row, lon, (lat, other), step).start()
        kv_copy(row, lon, (lat, sibling), 0).start()

    def kv_forward(row):
        for step in range(1, chips):
            owner = lax.rem(lon + lon_size - 2 * step, lon_size)
            kv_copy(row, owner, (lat, sibling), 0).wait_recv()
            kv_copy(row, owner, (lat, sibling), chips - 1 + step).start()

    def kv_collect(row):
        for step in range(chips):
            owner = lax.rem(sibling + lon_size - 2 * step, lon_size)
            kv_copy(row, owner, (lat, sibling), 0).wait_recv()

    def mixed_copy(row):
        return pltpu.make_async_copy(mixed_field.at[row], mixed_out.at[row], out_sem.at[0, row])

    def attended_copy(row):
        return pltpu.make_async_copy(attended.at[row], attended_out.at[row], out_sem.at[1, row])

    def project(first, step, count):
        def one(index, carry):
            row = first + index * step
            tokens = mixed_field[row].astype(jnp.float32)
            mean_square = jnp.mean(tokens * tokens, axis=-1, keepdims=True)
            scaled = tokens * lax.rsqrt(mean_square + 1e-06) * gain_ref[...]
            normed[row] = scaled.astype(jnp.bfloat16)
            key_values[row, own_columns(lon)] = jnp.dot(
                normed[row], key_value_weight[...], preferred_element_type=jnp.float32
            ).astype(jnp.bfloat16)
            kv_start(row)
            mixed_copy(row).start()
            return carry

        lax.fori_loop(0, count, one, 0)

    def attend_row(row):
        place_queries(normed[row], query_weight, placed)
        kv_collect(row)

        def store(g, value):
            attended[row, :, g * BLOCK : (g + 1) * BLOCK] = value

        attend(
            placed,
            lambda: key_values[row, :, :BLOCK],
            lambda: key_values[row, :, BLOCK:],
            mixed,
            store,
        )
        attended_copy(row).start()

    loads[0].wait()
    for side in sides:
        side.wait_recv()
    receive_halos((1, band + 2))
    stencil(wide, 2, 1, band, 2, stencil_one_ref, store_after_one)
    loads[1].wait()
    stencil(after_one, 2, 1, band - 2, 3, stencil_two_ref, store_mixed)
    project(1, 1, band - 2)
    loads[2].wait()
    kv_forward(1)
    attend_row(1)

    receive_halos((0, band + 3))
    stencil(wide, 1, band + 1, 2, 1, stencil_one_ref, store_after_one)
    stencil(after_one, 1, last, 2, 2, stencil_two_ref, store_mixed)
    project(0, last, 2)
    kv_forward(2)

    def one_row(index, carry):
        attend_row(lax.rem(index + 2, band))

        @pl.when(index < band - 2)
        def _():
            kv_forward(lax.rem(index + 3, band))

        return carry

    lax.fori_loop(0, band - 1, one_row, 0)

    far_top.wait_send()
    far_bottom.wait_send()
    for side in sides:
        side.wait_send()
    for row in (0, 1, band + 2, band + 3):
        for edge in edges(row):
            edge.wait_send()

    def finish(row, carry):
        for slot in range(lon_size - 1):
            kv_copy(row, lon, (lat, sibling), slot).wait_send()
        mixed_copy(row).wait()
        attended_copy(row).wait()
        return carry

    lax.fori_loop(0, band, finish, 0)


def local(grid_state, stencil_one, stencil_two, norm_gain, query_weight, key_value_weight):
    level_count, band, width, channels = grid_state.shape
    lat_size, lon_size = lax.axis_size("lat"), lax.axis_size("lon")
    circle = row_weights(lax.axis_index("lat") * band - 2, band + 4, band * lat_size)
    whole = pl.BlockSpec(memory_space=pltpu.VMEM)
    anywhere = pl.BlockSpec(memory_space=pl.ANY)
    field = jax.ShapeDtypeStruct((band, width, channels), jnp.bfloat16)
    wide_width = width + 2 * EDGE
    rows = (band, width, channels)
    dma = pltpu.SemaphoreType.DMA
    mixed_field, attended = pl.pallas_call(
        functools.partial(block_kernel, lat_size, lon_size),
        out_shape=(field, field),
        in_specs=[
            pl.BlockSpec(memory_space=pltpu.SMEM),
            anywhere,
            whole,
            whole,
            whole,
            anywhere,
            anywhere,
        ],
        out_specs=(anywhere, anywhere),
        scratch_shapes=[
            pltpu.VMEM((band + 4, wide_width, channels), jnp.bfloat16),
            pltpu.VMEM((band + 2, wide_width, channels), jnp.bfloat16),
            pltpu.VMEM(rows, jnp.bfloat16),
            pltpu.VMEM(rows, jnp.bfloat16),
            pltpu.VMEM((band, width * lon_size, 2 * BLOCK), jnp.bfloat16),
            pltpu.VMEM((GROUPS, KV_HEADS, width, BLOCK), jnp.bfloat16),
            pltpu.VMEM((GROUPS, width, BLOCK), jnp.float32),
            pltpu.VMEM(rows, jnp.bfloat16),
            pltpu.VMEM(query_weight.shape, jnp.bfloat16),
            pltpu.VMEM(key_value_weight.shape, jnp.bfloat16),
            dma((3,)),
            dma((2, band)),
            dma((4,)),
            dma((band + 4,)),
            dma((2,)),
            dma((2,)),
            dma((4, 2)),
            dma((4, 2)),
            dma((band, lon_size - 1)),
            dma((band, lon_size)),
        ],
        compiler_params=pltpu.CompilerParams(
            collective_id=0, has_side_effects=True, vmem_limit_bytes=56 * 1024 * 1024
        ),
    )(
        circle,
        grid_state[0],
        stencil_one,
        stencil_two,
        norm_gain[None],
        query_weight,
        key_value_weight,
    )
    return (mixed_field[None], attended[None])


def solution(mesh):
    in_specs = (P(None, "lat", "lon", None), P(), P(), P(), P(), P())
    out_specs = (P(None, "lat", "lon", None), P(None, "lat", "lon", None))
    return jax.shard_map(local, mesh=mesh, in_specs=in_specs, out_specs=out_specs, check_vma=False)
```

```python
import functools
import math

import jax
import jax.numpy as jnp
from jax import lax
from jax.experimental import pallas as pl
from jax.experimental.pallas import tpu as pltpu
from jax.sharding import PartitionSpec as P

HEADS = 16
KV_HEADS = 4
HEAD_DIM = 64
GROUPS = HEADS // KV_HEADS
BLOCK = KV_HEADS * HEAD_DIM
EDGE = 16
STENCIL_ONE_ROW, STENCIL_TWO_ROW, GAIN_ROW, CIRCLE_ROW = 0, 6, 12, 13
MESH = pl.DeviceIdType.MESH
QUERY_SCALE = math.log2(math.e) / math.sqrt(HEAD_DIM)


def lane_group(shape):
    return lax.broadcasted_iota(jnp.int32, shape, len(shape) - 1) // HEAD_DIM


def place_queries(normed, query_weight_ref, placed_ref):
    for g in range(KV_HEADS):
        weight = query_weight_ref[:, g * BLOCK : (g + 1) * BLOCK]
        block = jnp.dot(normed, weight, preferred_element_type=jnp.float32) * QUERY_SCALE
        group = lane_group(block.shape)
        for j in range(GROUPS):
            shift = (g - j) * HEAD_DIM % BLOCK
            moved = pltpu.roll(block, shift, 1) if shift else block
            placed_ref[j, g] = jnp.where(group == g, moved, 0.0).astype(jnp.bfloat16)


def attend(placed_ref, keys_ref, values_ref, mixed_ref, store):
    owners = range(keys_ref.shape[0])
    heads = [(j, g) for j in range(GROUPS) for g in range(KV_HEADS)]

    def scores_of(head):
        query = placed_ref[head]
        return [
            jnp.dot(query, keys_ref[o], preferred_element_type=jnp.float32) for o in owners
        ]

    scores = scores_of(heads[0])
    for index, (j, g) in enumerate(heads):
        following = scores_of(heads[index + 1]) if index + 1 < len(heads) else None
        peak = jnp.max(functools.reduce(jnp.maximum, scores), axis=-1, keepdims=True)
        probs = [jnp.exp2(part - peak) for part in scores]
        denominator = jnp.sum(sum(probs[1:], probs[0]), axis=-1, keepdims=True)
        updates = [
            jnp.dot(probs[o].astype(jnp.bfloat16), values_ref[o], preferred_element_type=jnp.float32)
            for o in owners
        ]
        update = sum(updates[1:], updates[0]) / denominator
        if g == 0:
            mixed = update
        else:
            mixed = jnp.where(lane_group(update.shape) == g, update, mixed)
        if g == KV_HEADS - 1:
            mixed_ref[j] = mixed
        scores = following
    for g in range(KV_HEADS):
        out = jnp.zeros(mixed_ref.shape[1:], jnp.float32)
        group = lane_group(out.shape)
        for j in range(GROUPS):
            shift = (j - g) * HEAD_DIM % BLOCK
            part = mixed_ref[j]
            moved = pltpu.roll(part, shift, 1) if shift else part
            out = jnp.where(group == j, moved, out)
        store(g, out.astype(jnp.bfloat16))


def row_weights(first_row, row_count, nlat_total):
    positions = (jnp.arange(row_count, dtype=jnp.int32) + first_row).astype(jnp.float32)
    return jnp.abs(jnp.sin(jnp.pi * (positions + 0.5) / nlat_total))


def block_kernel(
    lat_size,
    lon_size,
    table_ref,
    grid_ref,
    query_hbm,
    key_value_hbm,
    mixed_out,
    attended_out,
    wide,
    after_one,
    mixed_field,
    normed,
    keys,
    values,
    placed,
    mixed,
    attended,
    query_weight,
    key_value_weight,
    local_sem,
    out_sem,
    halo_send,
    halo_recv,
    side_send,
    side_recv,
    edge_send,
    edge_recv,
    kv_send,
    kv_recv,
):
    band, width, channels = grid_ref.shape
    last = band - 1
    lat = lax.axis_index("lat")
    lon = lax.axis_index("lon")
    chips = lon_size // 2
    left, right = lax.rem(lon + lon_size - 1, lon_size), lax.rem(lon + 1, lon_size)
    sibling = lon + 1 - 2 * lax.rem(lon, 2)
    partner = lax.rem(lon + lon_size // 2, lon_size)
    top = (jnp.where(lat == 0, lat, lat - 1), jnp.where(lat == 0, partner, lon))
    at_end = lat == lat_size - 1
    bottom = (jnp.where(at_end, lat, lat + 1), jnp.where(at_end, partner, lon))

    def remote(src, dst, send, recv, device):
        return pltpu.make_async_remote_copy(
            src_ref=src,
            dst_ref=dst,
            send_sem=send,
            recv_sem=recv,
            device_id=device,
            device_id_type=MESH,
        )

    loads = [
        pltpu.make_async_copy(
            grid_ref, wide.at[pl.ds(2, band), pl.ds(EDGE, width)], local_sem.at[0]
        ),
        pltpu.make_async_copy(key_value_hbm, key_value_weight, local_sem.at[1]),
        pltpu.make_async_copy(query_hbm, query_weight, local_sem.at[2]),
    ]
    for load in loads:
        load.start()

    barrier = pltpu.get_barrier_semaphore()
    for device in (top, bottom):
        pl.semaphore_signal(barrier, inc=1, device_id=device, device_id_type=MESH)
    for step in range(1, lon_size):
        other = (lat, lax.rem(lon + step, lon_size))
        pl.semaphore_signal(barrier, inc=1, device_id=other, device_id_type=MESH)
    pl.semaphore_wait(barrier, lon_size + 1)

    def from_top(stage):
        return lax.rem(lat + stage, 2) == 1

    def halo_row(stage):
        far = stage // 2
        return jnp.where(from_top(stage), 1 - far, band + 2 + far)

    def mixed_row(stage):
        near = 1 - stage // 2
        return jnp.where(from_top(stage), near, last - near)

    def halo_copy(stage):
        far = stage // 2
        up = from_top(stage)
        pole = lat == jnp.where(up, 0, lat_size - 1)
        source = jnp.where(up, far, last - far)
        target = jnp.where(up == pole, 1 - far, band + 2 + far)
        device = (
            jnp.where(pole, lat, jnp.where(up, lat - 1, lat + 1)),
            jnp.where(pole, partner, lon),
        )
        return remote(
            grid_ref.at[source],
            wide.at[target, pl.ds(EDGE, width)],
            halo_send.at[stage],
            halo_recv.at[stage],
            device,
        )

    def halo_arrival(stage):
        block = wide.at[halo_row(stage), pl.ds(EDGE, width)]
        return remote(block, block, halo_send.at[stage], halo_recv.at[stage], (lat, sibling))

    sides = [
        remote(
            grid_ref.at[:, pl.ds(width - EDGE, EDGE)],
            wide.at[pl.ds(2, band), pl.ds(0, EDGE)],
            side_send.at[0],
            side_recv.at[0],
            (lat, right),
        ),
        remote(
            grid_ref.at[:, pl.ds(0, EDGE)],
            wide.at[pl.ds(2, band), pl.ds(EDGE + width, EDGE)],
            side_send.at[1],
            side_recv.at[1],
            (lat, left),
        ),
    ]
    for side in sides:
        side.start()
    halo_copy(0).start()

    def edges(stage):
        row = halo_row(stage)
        return [
            remote(
                wide.at[row, pl.ds(width, EDGE)],
                wide.at[row, pl.ds(0, EDGE)],
                edge_send.at[stage, 0],
                edge_recv.at[stage, 0],
                (lat, right),
            ),
            remote(
                wide.at[row, pl.ds(EDGE, EDGE)],
                wide.at[row, pl.ds(EDGE + width, EDGE)],
                edge_send.at[stage, 1],
                edge_recv.at[stage, 1],
                (lat, left),
            ),
        ]

    def stencil(source, first, count, circle_first, weights_first, store):
        total = width + 2 * EDGE
        chunks = channels // 128

        def one(index, carry):
            row = first + index // chunks
            circle = CIRCLE_ROW + circle_first + index // chunks
            lanes = pl.ds(pl.multiple_of(index % chunks * 128, 128), 128)
            above = source[row - 1, :, lanes].astype(jnp.float32)
            centre = source[row, :, lanes].astype(jnp.float32)
            below = source[row + 1, :, lanes].astype(jnp.float32)
            above_factor = table_ref[circle - 1, :, lanes]
            own_factor = table_ref[circle, :, lanes]
            below_factor = table_ref[circle + 1, :, lanes]
            beside = above_factor * above + below_factor * below
            taps = []
            for offset in range(3):
                own = table_ref[weights_first + offset, :, lanes] * own_factor
                next_to = table_ref[weights_first + 3 + offset, :, lanes]
                taps.append(own * centre + next_to * beside)
            result = centre + taps[1] + pltpu.roll(taps[0], 1, 0)
            result = result + pltpu.roll(taps[2], total - 1, 0)
            store(row, lanes, result.astype(jnp.bfloat16))
            return carry

        lax.fori_loop(0, count * chunks, one, 0)

    def store_after_one(row, lanes, value):
        after_one[row - 1, :, lanes] = value

    def store_mixed(row, lanes, value):
        mixed_field[row - 1, :, lanes] = value[EDGE : EDGE + width]

    def kv_copies(row, owner, device, slot):
        return [
            remote(
                held.at[row, owner],
                held.at[row, owner],
                kv_send.at[kind, row, slot],
                kv_recv.at[kind, row, owner],
                device,
            )
            for kind, held in enumerate((keys, values))
        ]

    def kv_start(row):
        for step in range(1, chips):
            for copy in kv_copies(row, lon, (lat, lax.rem(lon + 2 * step, lon_size)), step):
                copy.start()
        for copy in kv_copies(row, lon, (lat, sibling), 0):
            copy.start()

    def kv_forward(row):
        for step in range(1, chips):
            owner = lax.rem(lon + lon_size - 2 * step, lon_size)
            for copy in kv_copies(row, owner, (lat, sibling), chips - 1 + step):
                copy.wait_recv()
                copy.start()

    def kv_collect(row):
        for step in range(chips):
            owner = lax.rem(sibling + lon_size - 2 * step, lon_size)
            for copy in kv_copies(row, owner, (lat, sibling), 0):
                copy.wait_recv()

    def mixed_copy(row):
        return pltpu.make_async_copy(mixed_field.at[row], mixed_out.at[row], out_sem.at[0, row])

    def attended_copy(row):
        return pltpu.make_async_copy(attended.at[row], attended_out.at[row], out_sem.at[1, row])

    def project(row):
        tokens = mixed_field[row].astype(jnp.float32)
        mean_square = jnp.mean(tokens * tokens, axis=-1, keepdims=True)
        scaled = tokens * lax.rsqrt(mean_square + 1e-06) * table_ref[GAIN_ROW]
        normed[row] = scaled.astype(jnp.bfloat16)
        both = jnp.dot(normed[row], key_value_weight[...], preferred_element_type=jnp.float32)
        keys[row, lon] = jnp.transpose(both[:, :BLOCK]).astype(jnp.bfloat16)
        values[row, lon] = both[:, BLOCK:].astype(jnp.bfloat16)
        kv_start(row)
        mixed_copy(row).start()

    def attend_row(row):
        kv_forward(row)
        place_queries(normed[row], query_weight, placed)
        kv_collect(row)

        def store(g, value):
            attended[row, :, g * BLOCK : (g + 1) * BLOCK] = value

        attend(placed, keys.at[row], values.at[row], mixed, store)
        attended_copy(row).start()

    loads[0].wait()
    for side in sides:
        side.wait_recv()
    stencil(wide, 3, band - 2, 3, STENCIL_ONE_ROW, store_after_one)
    loads[1].wait()
    loads[2].wait()

    def one_stage(stage, carry):
        @pl.when(stage < band)
        def _():
            halo_copy(stage).wait_send()

            @pl.when(stage < band - 1)
            def _():
                halo_copy(stage + 1).start()

            halo_arrival(stage).wait_recv()
            for edge in edges(stage):
                edge.start()
            for edge in edges(stage):
                edge.wait_recv()
            row = mixed_row(stage)
            outer = jnp.where(from_top(stage), row + 1, row + 3)
            stencil(wide, outer, 1, outer, STENCIL_ONE_ROW, store_after_one)
            stencil(after_one, row + 1, 1, row + 2, STENCIL_TWO_ROW, store_mixed)
            project(row)

        @pl.when(stage > 0)
        def _():
            attend_row(mixed_row(stage - 1))

        return carry

    lax.fori_loop(0, band + 1, one_stage, 0)

    for side in sides:
        side.wait_send()

    def finish(row, carry):
        for edge in edges(row):
            edge.wait_send()
        for slot in range(lon_size - 1):
            for copy in kv_copies(row, lon, (lat, sibling), slot):
                copy.wait_send()
        mixed_copy(row).wait()
        attended_copy(row).wait()
        return carry

    lax.fori_loop(0, band, finish, 0)


def local(grid_state, stencil_one, stencil_two, norm_gain, query_weight, key_value_weight):
    level_count, band, width, channels = grid_state.shape
    lat_size, lon_size = lax.axis_size("lat"), lax.axis_size("lon")
    circle = row_weights(lax.axis_index("lat") * band - 2, band + 4, band * lat_size)
    table = jnp.concatenate(
        [
            stencil_one.reshape(6, channels),
            stencil_two.reshape(6, channels),
            norm_gain[None],
            jnp.broadcast_to(circle[:, None], (band + 4, channels)),
        ]
    )[:, None]
    whole = pl.BlockSpec(memory_space=pltpu.VMEM)
    anywhere = pl.BlockSpec(memory_space=pl.ANY)
    field = jax.ShapeDtypeStruct((band, width, channels), jnp.bfloat16)
    wide_width = width + 2 * EDGE
    rows = (band, width, channels)
    dma = pltpu.SemaphoreType.DMA
    mixed_field, attended = pl.pallas_call(
        functools.partial(block_kernel, lat_size, lon_size),
        out_shape=(field, field),
        in_specs=[
            whole,
            anywhere,
            anywhere,
            anywhere,
        ],
        out_specs=(anywhere, anywhere),
        scratch_shapes=[
            pltpu.VMEM((band + 4, wide_width, channels), jnp.bfloat16),
            pltpu.VMEM((band + 2, wide_width, channels), jnp.bfloat16),
            pltpu.VMEM(rows, jnp.bfloat16),
            pltpu.VMEM(rows, jnp.bfloat16),
            pltpu.VMEM((band, lon_size, BLOCK, width), jnp.bfloat16),
            pltpu.VMEM((band, lon_size, width, BLOCK), jnp.bfloat16),
            pltpu.VMEM((GROUPS, KV_HEADS, width, BLOCK), jnp.bfloat16),
            pltpu.VMEM((GROUPS, width, BLOCK), jnp.float32),
            pltpu.VMEM(rows, jnp.bfloat16),
            pltpu.VMEM(query_weight.shape, jnp.bfloat16),
            pltpu.VMEM(key_value_weight.shape, jnp.bfloat16),
            dma((3,)),
            dma((2, band)),
            dma((4,)),
            dma((4,)),
            dma((2,)),
            dma((2,)),
            dma((4, 2)),
            dma((4, 2)),
            dma((2, band, lon_size - 1)),
            dma((2, band, lon_size)),
        ],
        compiler_params=pltpu.CompilerParams(
            collective_id=0, has_side_effects=True, vmem_limit_bytes=56 * 1024 * 1024
        ),
    )(
        table,
        grid_state[0],
        query_weight,
        key_value_weight,
    )
    return (mixed_field[None], attended[None])


def solution(mesh):
    in_specs = (P(None, "lat", "lon", None), P(), P(), P(), P(), P())
    out_specs = (P(None, "lat", "lon", None), P(None, "lat", "lon", None))
    return jax.shard_map(local, mesh=mesh, in_specs=in_specs, out_specs=out_specs, check_vma=False)
```

```python
import functools
import math

import jax
import jax.numpy as jnp
from jax import lax
from jax.experimental import pallas as pl
from jax.experimental.pallas import tpu as pltpu
from jax.sharding import PartitionSpec as P

HEADS = 16
KV_HEADS = 4
HEAD_DIM = 64
GROUPS = HEADS // KV_HEADS
BLOCK = KV_HEADS * HEAD_DIM
EDGE = 16
STENCIL_ONE_ROW, STENCIL_TWO_ROW, GAIN_ROW = 0, 6, 12
MESH = pl.DeviceIdType.MESH
QUERY_SCALE = math.log2(math.e) / math.sqrt(HEAD_DIM)


def lane_group(shape):
    return lax.broadcasted_iota(jnp.int32, shape, len(shape) - 1) // HEAD_DIM


def place_queries(normed, query_weight_ref, placed_ref):
    for g in range(KV_HEADS):
        weight = query_weight_ref[:, g * BLOCK : (g + 1) * BLOCK]
        block = jnp.dot(normed, weight, preferred_element_type=jnp.float32) * QUERY_SCALE
        group = lane_group(block.shape)
        for j in range(GROUPS):
            shift = (g - j) * HEAD_DIM % BLOCK
            moved = pltpu.roll(block, shift, 1) if shift else block
            placed_ref[j, g] = jnp.where(group == g, moved, 0.0).astype(jnp.bfloat16)


def attend(placed_ref, keys_ref, values_ref, mixed_ref, store):
    owners = range(keys_ref.shape[0])
    columns = keys_ref.shape[0] * keys_ref.shape[2]
    heads = [(j, g) for j in range(GROUPS) for g in range(KV_HEADS)]

    def scores_of(head):
        query = placed_ref[head]
        return [
            jnp.dot(query, keys_ref[o], preferred_element_type=jnp.float32) for o in owners
        ]

    scores = scores_of(heads[0])
    for index, (j, g) in enumerate(heads):
        following = scores_of(heads[index + 1]) if index + 1 < len(heads) else None
        peak = jnp.max(functools.reduce(jnp.maximum, scores), axis=-1, keepdims=True)
        probs = [jnp.exp2(part - peak) for part in scores]
        denominator = jnp.sum(sum(probs[1:], probs[0]), axis=-1, keepdims=True)
        rounded = jnp.concatenate([part.astype(jnp.bfloat16) for part in probs], axis=1)
        update = jnp.dot(
            rounded, values_ref[...].reshape(columns, BLOCK), preferred_element_type=jnp.float32
        ) * (1.0 / denominator)
        if g == 0:
            mixed = update
        else:
            mixed = jnp.where(lane_group(update.shape) == g, update, mixed)
        if g == KV_HEADS - 1:
            mixed_ref[j] = mixed
        scores = following
    for g in range(KV_HEADS):
        out = jnp.zeros(mixed_ref.shape[1:], jnp.float32)
        group = lane_group(out.shape)
        for j in range(GROUPS):
            shift = (j - g) * HEAD_DIM % BLOCK
            part = mixed_ref[j]
            moved = pltpu.roll(part, shift, 1) if shift else part
            out = jnp.where(group == j, moved, out)
        store(g, out.astype(jnp.bfloat16))


def block_kernel(
    lat_size,
    lon_size,
    table_ref,
    grid_ref,
    query_hbm,
    key_value_hbm,
    mixed_out,
    attended_out,
    wide,
    after_one,
    mixed_field,
    normed,
    keys,
    values,
    placed,
    mixed,
    attended,
    query_weight,
    key_value_weight,
    circle_ref,
    local_sem,
    out_sem,
    halo_send,
    halo_recv,
    side_send,
    side_recv,
    edge_send,
    edge_recv,
    kv_send,
    kv_recv,
):
    band, width, channels = grid_ref.shape
    last = band - 1
    lat = lax.axis_index("lat")
    lon = lax.axis_index("lon")
    chips = lon_size // 2
    left, right = lax.rem(lon + lon_size - 1, lon_size), lax.rem(lon + 1, lon_size)
    sibling = lon + 1 - 2 * lax.rem(lon, 2)
    partner = lax.rem(lon + lon_size // 2, lon_size)
    top = (jnp.where(lat == 0, lat, lat - 1), jnp.where(lat == 0, partner, lon))
    at_end = lat == lat_size - 1
    bottom = (jnp.where(at_end, lat, lat + 1), jnp.where(at_end, partner, lon))

    def remote(src, dst, send, recv, device):
        return pltpu.make_async_remote_copy(
            src_ref=src,
            dst_ref=dst,
            send_sem=send,
            recv_sem=recv,
            device_id=device,
            device_id_type=MESH,
        )

    loads = [
        pltpu.make_async_copy(
            grid_ref, wide.at[pl.ds(2, band), pl.ds(EDGE, width)], local_sem.at[0]
        ),
        pltpu.make_async_copy(key_value_hbm, key_value_weight, local_sem.at[1]),
        pltpu.make_async_copy(query_hbm, query_weight, local_sem.at[2]),
    ]
    for load in loads:
        load.start()

    barrier = pltpu.get_barrier_semaphore()
    for device in (top, bottom):
        pl.semaphore_signal(barrier, inc=1, device_id=device, device_id_type=MESH)
    for step in range(1, lon_size):
        other = (lat, lax.rem(lon + step, lon_size))
        pl.semaphore_signal(barrier, inc=1, device_id=other, device_id_type=MESH)
    pl.semaphore_wait(barrier, lon_size + 1)

    def from_top(stage):
        return lax.rem(lat + stage, 2) == 1

    def halo_row(stage):
        far = stage // 2
        return jnp.where(from_top(stage), 1 - far, band + 2 + far)

    def mixed_row(stage):
        near = 1 - stage // 2
        return jnp.where(from_top(stage), near, last - near)

    def halo_copy(stage):
        far = stage // 2
        up = from_top(stage)
        pole = lat == jnp.where(up, 0, lat_size - 1)
        source = jnp.where(up, far, last - far)
        target = jnp.where(up == pole, 1 - far, band + 2 + far)
        device = (
            jnp.where(pole, lat, jnp.where(up, lat - 1, lat + 1)),
            jnp.where(pole, partner, lon),
        )
        return remote(
            grid_ref.at[source],
            wide.at[target, pl.ds(EDGE, width)],
            halo_send.at[stage],
            halo_recv.at[stage],
            device,
        )

    def halo_arrival(stage):
        block = wide.at[halo_row(stage), pl.ds(EDGE, width)]
        return remote(block, block, halo_send.at[stage], halo_recv.at[stage], (lat, sibling))

    sides = [
        remote(
            grid_ref.at[:, pl.ds(width - EDGE, EDGE)],
            wide.at[pl.ds(2, band), pl.ds(0, EDGE)],
            side_send.at[0],
            side_recv.at[0],
            (lat, right),
        ),
        remote(
            grid_ref.at[:, pl.ds(0, EDGE)],
            wide.at[pl.ds(2, band), pl.ds(EDGE + width, EDGE)],
            side_send.at[1],
            side_recv.at[1],
            (lat, left),
        ),
    ]
    for side in sides:
        side.start()
    halo_copy(0).start()

    at_pole = jnp.logical_or(lat == 0, at_end)

    @pl.when(at_pole)
    def _():
        halo_copy(1).start()

    def edges(stage):
        row = halo_row(stage)
        return [
            remote(
                wide.at[row, pl.ds(width, EDGE)],
                wide.at[row, pl.ds(0, EDGE)],
                edge_send.at[stage, 0],
                edge_recv.at[stage, 0],
                (lat, right),
            ),
            remote(
                wide.at[row, pl.ds(EDGE, EDGE)],
                wide.at[row, pl.ds(EDGE + width, EDGE)],
                edge_send.at[stage, 1],
                edge_recv.at[stage, 1],
                (lat, left),
            ),
        ]

    def stencil(source, first, count, circle_first, weights_first, store, strips):
        chunks = channels // 128

        def one(index, carry):
            row = first + index // chunks
            circle = circle_first + index // chunks
            lanes = pl.ds(pl.multiple_of(index % chunks * 128, 128), 128)
            factors = [circle_ref[circle + offset] for offset in (-1, 0, 1)]
            own = [
                table_ref[weights_first + offset, :, lanes] * factors[1] for offset in range(3)
            ]
            next_to = [table_ref[weights_first + 3 + offset, :, lanes] for offset in range(3)]

            def taps(strip):
                columns = pl.ds(strip * EDGE, EDGE)
                above = source[row - 1, columns, lanes].astype(jnp.float32)
                centre = source[row, columns, lanes].astype(jnp.float32)
                below = source[row + 1, columns, lanes].astype(jnp.float32)
                beside = factors[0] * above + factors[2] * below
                parts = [own[offset] * centre + next_to[offset] * beside for offset in range(3)]
                return parts[0], centre + parts[1], parts[2]

            start, stop = strips
            before, here = taps(max(start - 1, 0)), taps(start)
            for strip in range(start, stop):
                after = taps(min(strip + 1, width // EDGE + 1))
                west = jnp.concatenate([before[0][8:], here[0]], axis=0)
                east = jnp.concatenate([here[2], after[2][:8]], axis=0)
                result = here[1] + pltpu.roll(west, 1, 0)[8:] + pltpu.roll(east, 23, 0)[:EDGE]
                store(row, strip, lanes, result.astype(jnp.bfloat16))
                before, here = here, after
            return carry

        lax.fori_loop(0, count * chunks, one, 0)

    inner = (1, width // EDGE + 1)
    outward = (0, width // EDGE + 2)

    def store_after_one(row, strip, lanes, value):
        after_one[row - 1, pl.ds(strip * EDGE, EDGE), lanes] = value

    def store_mixed(row, strip, lanes, value):
        mixed_field[row - 1, pl.ds((strip - 1) * EDGE, EDGE), lanes] = value

    def kv_copies(row, owner, device, slot):
        return [
            remote(
                held.at[row, owner],
                held.at[row, owner],
                kv_send.at[kind, row, slot],
                kv_recv.at[kind, row, owner],
                device,
            )
            for kind, held in enumerate((keys, values))
        ]

    def kv_start(row):
        for step in range(1, chips):
            for copy in kv_copies(row, lon, (lat, lax.rem(lon + 2 * step, lon_size)), step):
                copy.start()
        for copy in kv_copies(row, lon, (lat, sibling), 0):
            copy.start()

    def kv_forward(row):
        for step in range(1, chips):
            owner = lax.rem(lon + lon_size - 2 * step, lon_size)
            for copy in kv_copies(row, owner, (lat, sibling), chips - 1 + step):
                copy.wait_recv()
                copy.start()

    def kv_collect(row):
        for step in range(chips):
            owner = lax.rem(sibling + lon_size - 2 * step, lon_size)
            for copy in kv_copies(row, owner, (lat, sibling), 0):
                copy.wait_recv()

    def mixed_copy(row):
        return pltpu.make_async_copy(mixed_field.at[row], mixed_out.at[row], out_sem.at[0, row])

    def attended_copy(row):
        return pltpu.make_async_copy(attended.at[row], attended_out.at[row], out_sem.at[1, row])

    def project(row):
        tokens = mixed_field[row].astype(jnp.float32)
        mean_square = jnp.mean(tokens * tokens, axis=-1, keepdims=True)
        scaled = tokens * lax.rsqrt(mean_square + 1e-06) * table_ref[GAIN_ROW]
        normed[row] = scaled.astype(jnp.bfloat16)
        both = jnp.dot(normed[row], key_value_weight[...], preferred_element_type=jnp.float32)
        keys[row, lon] = jnp.transpose(both[:, :BLOCK]).astype(jnp.bfloat16)
        values[row, lon] = both[:, BLOCK:].astype(jnp.bfloat16)
        kv_start(row)
        mixed_copy(row).start()

    def attend_row(row):
        kv_forward(row)
        place_queries(normed[row], query_weight, placed)
        kv_collect(row)

        def store(g, value):
            attended[row, :, g * BLOCK : (g + 1) * BLOCK] = value

        attend(placed, keys.at[row], values.at[row], mixed, store)
        attended_copy(row).start()

    positions = lax.broadcasted_iota(jnp.int32, circle_ref.shape, 0) + (lat * band - 2)
    angle = jnp.pi * (positions.astype(jnp.float32) + 0.5) / (band * lat_size)
    circle_ref[...] = jnp.abs(jnp.sin(angle))

    loads[0].wait()
    for side in sides:
        side.wait_recv()
    stencil(wide, 3, band - 2, 3, STENCIL_ONE_ROW, store_after_one, outward)
    loads[1].wait()
    loads[2].wait()

    def one_stage(stage, carry):
        @pl.when(stage < band)
        def _():
            @pl.when(at_pole)
            def _():
                @pl.when(stage == 0)
                def _():
                    halo_copy(0).wait_send()
                    halo_copy(1).wait_send()
                    halo_copy(3).start()

                @pl.when(stage == 1)
                def _():
                    halo_copy(2).start()

                @pl.when(stage > 1)
                def _():
                    halo_copy(stage).wait_send()

            @pl.when(jnp.logical_not(at_pole))
            def _():
                halo_copy(stage).wait_send()

                @pl.when(stage < band - 1)
                def _():
                    halo_copy(stage + 1).start()

            halo_arrival(stage).wait_recv()
            for edge in edges(stage):
                edge.start()
            for edge in edges(stage):
                edge.wait_recv()
            row = mixed_row(stage)
            outer = jnp.where(from_top(stage), row + 1, row + 3)
            stencil(wide, outer, 1, outer, STENCIL_ONE_ROW, store_after_one, outward)
            stencil(after_one, row + 1, 1, row + 2, STENCIL_TWO_ROW, store_mixed, inner)
            project(row)

        @pl.when(stage > 0)
        def _():
            attend_row(mixed_row(stage - 1))

        return carry

    lax.fori_loop(0, band + 1, one_stage, 0)

    for side in sides:
        side.wait_send()

    def finish(row, carry):
        for edge in edges(row):
            edge.wait_send()
        for slot in range(lon_size - 1):
            for copy in kv_copies(row, lon, (lat, sibling), slot):
                copy.wait_send()
        mixed_copy(row).wait()
        attended_copy(row).wait()
        return carry

    lax.fori_loop(0, band, finish, 0)


def local(grid_state, stencil_one, stencil_two, norm_gain, query_weight, key_value_weight):
    level_count, band, width, channels = grid_state.shape
    lat_size, lon_size = lax.axis_size("lat"), lax.axis_size("lon")
    table = jnp.stack(
        [stencil_one[a, b] for a in range(2) for b in range(3)]
        + [stencil_two[a, b] for a in range(2) for b in range(3)]
        + [norm_gain]
    )[:, None]
    whole = pl.BlockSpec(memory_space=pltpu.VMEM)
    anywhere = pl.BlockSpec(memory_space=pl.ANY)
    field = jax.ShapeDtypeStruct((band, width, channels), jnp.bfloat16)
    wide_width = width + 2 * EDGE
    rows = (band, width, channels)
    dma = pltpu.SemaphoreType.DMA
    mixed_field, attended = pl.pallas_call(
        functools.partial(block_kernel, lat_size, lon_size),
        out_shape=(field, field),
        in_specs=[
            whole,
            anywhere,
            anywhere,
            anywhere,
        ],
        out_specs=(anywhere, anywhere),
        scratch_shapes=[
            pltpu.VMEM((band + 4, wide_width, channels), jnp.bfloat16),
            pltpu.VMEM((band + 2, wide_width, channels), jnp.bfloat16),
            pltpu.VMEM(rows, jnp.bfloat16),
            pltpu.VMEM(rows, jnp.bfloat16),
            pltpu.VMEM((band, lon_size, BLOCK, width), jnp.bfloat16),
            pltpu.VMEM((band, lon_size, width, BLOCK), jnp.bfloat16),
            pltpu.VMEM((GROUPS, KV_HEADS, width, BLOCK), jnp.bfloat16),
            pltpu.VMEM((GROUPS, width, BLOCK), jnp.float32),
            pltpu.VMEM(rows, jnp.bfloat16),
            pltpu.VMEM(query_weight.shape, jnp.bfloat16),
            pltpu.VMEM(key_value_weight.shape, jnp.bfloat16),
            pltpu.VMEM((band + 4, 1, 128), jnp.float32),
            dma((3,)),
            dma((2, band)),
            dma((4,)),
            dma((4,)),
            dma((2,)),
            dma((2,)),
            dma((4, 2)),
            dma((4, 2)),
            dma((2, band, lon_size - 1)),
            dma((2, band, lon_size)),
        ],
        compiler_params=pltpu.CompilerParams(
            collective_id=0, has_side_effects=True, vmem_limit_bytes=56 * 1024 * 1024
        ),
    )(
        table,
        grid_state[0],
        query_weight,
        key_value_weight,
    )
    return (mixed_field[None], attended[None])


def solution(mesh):
    in_specs = (P(None, "lat", "lon", None), P(), P(), P(), P(), P())
    out_specs = (P(None, "lat", "lon", None), P(None, "lat", "lon", None))
    return jax.shard_map(local, mesh=mesh, in_specs=in_specs, out_specs=out_specs, check_vma=False)
```

```python
import functools
import math

import jax
import jax.numpy as jnp
from jax import lax
from jax.experimental import pallas as pl
from jax.experimental.pallas import tpu as pltpu
from jax.sharding import PartitionSpec as P

HEADS = 16
KV_HEADS = 4
HEAD_DIM = 64
GROUPS = HEADS // KV_HEADS
BLOCK = KV_HEADS * HEAD_DIM
EDGE = 16
STENCIL_ONE_ROW, STENCIL_TWO_ROW, GAIN_ROW = 0, 6, 12
MESH = pl.DeviceIdType.MESH
QUERY_SCALE = math.log2(math.e) / math.sqrt(HEAD_DIM)
BUNDLE = 2


def lane_group(shape):
    return lax.broadcasted_iota(jnp.int32, shape, len(shape) - 1) // HEAD_DIM


def place_queries(normed, query_weight_ref, placed_ref):
    for g in range(KV_HEADS):
        weight = query_weight_ref[:, g * BLOCK : (g + 1) * BLOCK]
        block = jnp.dot(normed, weight, preferred_element_type=jnp.float32) * QUERY_SCALE
        group = lane_group(block.shape)
        for j in range(GROUPS):
            shift = (g - j) * HEAD_DIM % BLOCK
            moved = pltpu.roll(block, shift, 1) if shift else block
            placed_ref[j, g] = jnp.where(group == g, moved, 0.0).astype(jnp.bfloat16)


def attend(placed_ref, keys_ref, values_ref, mixed_ref, store):
    owners = range(keys_ref.shape[0])
    columns = keys_ref.shape[0] * keys_ref.shape[2]
    width = mixed_ref.shape[1]
    bundles = [(j, g) for j in range(GROUPS) for g in range(0, KV_HEADS, BUNDLE)]

    def scores_of(bundle):
        j, g = bundle
        query = placed_ref[j, g : g + BUNDLE].reshape(BUNDLE * width, BLOCK)
        return [
            jnp.dot(query, keys_ref[o], preferred_element_type=jnp.float32) for o in owners
        ]

    scores = scores_of(bundles[0])
    for index, (j, first) in enumerate(bundles):
        following = scores_of(bundles[index + 1]) if index + 1 < len(bundles) else None
        peak = jnp.max(functools.reduce(jnp.maximum, scores), axis=-1, keepdims=True)
        probs = [jnp.exp2(part - peak) for part in scores]
        denominator = jnp.sum(sum(probs[1:], probs[0]), axis=-1, keepdims=True)
        rounded = jnp.concatenate([part.astype(jnp.bfloat16) for part in probs], axis=1)
        update = jnp.dot(
            rounded, values_ref[...].reshape(columns, BLOCK), preferred_element_type=jnp.float32
        ) * (1.0 / denominator)
        for g in range(first, first + BUNDLE):
            part = update[(g - first) * width : (g - first + 1) * width]
            mixed = part if g == 0 else jnp.where(lane_group(part.shape) == g, part, mixed)
        if first + BUNDLE == KV_HEADS:
            mixed_ref[j] = mixed
        scores = following
    for g in range(KV_HEADS):
        out = jnp.zeros(mixed_ref.shape[1:], jnp.float32)
        group = lane_group(out.shape)
        for j in range(GROUPS):
            shift = (j - g) * HEAD_DIM % BLOCK
            part = mixed_ref[j]
            moved = pltpu.roll(part, shift, 1) if shift else part
            out = jnp.where(group == j, moved, out)
        store(g, out.astype(jnp.bfloat16))


def block_kernel(
    lat_size,
    lon_size,
    table_ref,
    grid_ref,
    query_hbm,
    key_value_hbm,
    mixed_out,
    attended_out,
    wide,
    after_one,
    mixed_field,
    normed,
    keys,
    values,
    placed,
    mixed,
    attended,
    query_weight,
    key_value_weight,
    circle_ref,
    local_sem,
    out_sem,
    halo_send,
    halo_recv,
    side_send,
    side_recv,
    edge_send,
    edge_recv,
    kv_send,
    kv_recv,
):
    band, width, channels = grid_ref.shape
    last = band - 1
    lat = lax.axis_index("lat")
    lon = lax.axis_index("lon")
    chips = lon_size // 2
    left, right = lax.rem(lon + lon_size - 1, lon_size), lax.rem(lon + 1, lon_size)
    sibling = lon + 1 - 2 * lax.rem(lon, 2)
    partner = lax.rem(lon + lon_size // 2, lon_size)
    top = (jnp.where(lat == 0, lat, lat - 1), jnp.where(lat == 0, partner, lon))
    at_end = lat == lat_size - 1
    bottom = (jnp.where(at_end, lat, lat + 1), jnp.where(at_end, partner, lon))

    def remote(src, dst, send, recv, device):
        return pltpu.make_async_remote_copy(
            src_ref=src,
            dst_ref=dst,
            send_sem=send,
            recv_sem=recv,
            device_id=device,
            device_id_type=MESH,
        )

    loads = [
        pltpu.make_async_copy(
            grid_ref, wide.at[pl.ds(2, band), pl.ds(EDGE, width)], local_sem.at[0]
        ),
        pltpu.make_async_copy(key_value_hbm, key_value_weight, local_sem.at[1]),
        pltpu.make_async_copy(query_hbm, query_weight, local_sem.at[2]),
    ]
    for load in loads:
        load.start()

    barrier = pltpu.get_barrier_semaphore()
    for device in (top, bottom):
        pl.semaphore_signal(barrier, inc=1, device_id=device, device_id_type=MESH)
    for step in range(1, lon_size):
        other = (lat, lax.rem(lon + step, lon_size))
        pl.semaphore_signal(barrier, inc=1, device_id=other, device_id_type=MESH)
    pl.semaphore_wait(barrier, lon_size + 1)

    def from_top(stage):
        return lax.rem(lat + stage, 2) == 1

    def halo_row(stage):
        far = stage // 2
        return jnp.where(from_top(stage), 1 - far, band + 2 + far)

    def mixed_row(stage):
        near = 1 - stage // 2
        return jnp.where(from_top(stage), near, last - near)

    def halo_copy(stage):
        far = stage // 2
        up = from_top(stage)
        pole = lat == jnp.where(up, 0, lat_size - 1)
        source = jnp.where(up, far, last - far)
        target = jnp.where(up == pole, 1 - far, band + 2 + far)
        device = (
            jnp.where(pole, lat, jnp.where(up, lat - 1, lat + 1)),
            jnp.where(pole, partner, lon),
        )
        return remote(
            grid_ref.at[source],
            wide.at[target, pl.ds(EDGE, width)],
            halo_send.at[stage],
            halo_recv.at[stage],
            device,
        )

    def halo_arrival(stage):
        block = wide.at[halo_row(stage), pl.ds(EDGE, width)]
        return remote(block, block, halo_send.at[stage], halo_recv.at[stage], (lat, sibling))

    sides = [
        remote(
            grid_ref.at[:, pl.ds(width - EDGE, EDGE)],
            wide.at[pl.ds(2, band), pl.ds(0, EDGE)],
            side_send.at[0],
            side_recv.at[0],
            (lat, right),
        ),
        remote(
            grid_ref.at[:, pl.ds(0, EDGE)],
            wide.at[pl.ds(2, band), pl.ds(EDGE + width, EDGE)],
            side_send.at[1],
            side_recv.at[1],
            (lat, left),
        ),
    ]
    for side in sides:
        side.start()
    halo_copy(0).start()

    at_pole = jnp.logical_or(lat == 0, at_end)

    @pl.when(at_pole)
    def _():
        halo_copy(1).start()

    def edges(stage):
        row = halo_row(stage)
        return [
            remote(
                wide.at[row, pl.ds(width, EDGE)],
                wide.at[row, pl.ds(0, EDGE)],
                edge_send.at[stage, 0],
                edge_recv.at[stage, 0],
                (lat, right),
            ),
            remote(
                wide.at[row, pl.ds(EDGE, EDGE)],
                wide.at[row, pl.ds(EDGE + width, EDGE)],
                edge_send.at[stage, 1],
                edge_recv.at[stage, 1],
                (lat, left),
            ),
        ]

    def stencil(source, first, count, circle_first, weights_first, store, strips):
        chunks = channels // 128

        def one(index, carry):
            row = first + index // chunks
            circle = circle_first + index // chunks
            lanes = pl.ds(pl.multiple_of(index % chunks * 128, 128), 128)
            factors = [circle_ref[circle + offset] for offset in (-1, 0, 1)]
            own = [
                table_ref[weights_first + offset, :, lanes] * factors[1] for offset in range(3)
            ]
            next_to = [table_ref[weights_first + 3 + offset, :, lanes] for offset in range(3)]

            def taps(strip):
                columns = pl.ds(strip * EDGE, EDGE)
                above = source[row - 1, columns, lanes].astype(jnp.float32)
                centre = source[row, columns, lanes].astype(jnp.float32)
                below = source[row + 1, columns, lanes].astype(jnp.float32)
                beside = factors[0] * above + factors[2] * below
                parts = [own[offset] * centre + next_to[offset] * beside for offset in range(3)]
                return parts[0], centre + parts[1], parts[2]

            start, stop = strips
            before, here = taps(max(start - 1, 0)), taps(start)
            for strip in range(start, stop):
                after = taps(min(strip + 1, width // EDGE + 1))
                west = jnp.concatenate([before[0][8:], here[0]], axis=0)
                east = jnp.concatenate([here[2], after[2][:8]], axis=0)
                result = here[1] + pltpu.roll(west, 1, 0)[8:] + pltpu.roll(east, 23, 0)[:EDGE]
                store(row, strip, lanes, result.astype(jnp.bfloat16))
                before, here = here, after
            return carry

        lax.fori_loop(0, count * chunks, one, 0)

    inner = (1, width // EDGE + 1)
    outward = (0, width // EDGE + 2)

    def store_after_one(row, strip, lanes, value):
        after_one[row - 1, pl.ds(strip * EDGE, EDGE), lanes] = value

    def store_mixed(row, strip, lanes, value):
        mixed_field[row - 1, pl.ds((strip - 1) * EDGE, EDGE), lanes] = value

    def kv_copies(row, owner, device, slot):
        return [
            remote(
                held.at[row, owner],
                held.at[row, owner],
                kv_send.at[kind, row, slot],
                kv_recv.at[kind, row, owner],
                device,
            )
            for kind, held in enumerate((keys, values))
        ]

    def kv_start(row):
        for step in range(1, chips):
            for copy in kv_copies(row, lon, (lat, lax.rem(lon + 2 * step, lon_size)), step):
                copy.start()
        for copy in kv_copies(row, lon, (lat, sibling), 0):
            copy.start()

    def kv_forward(row):
        for step in range(1, chips):
            owner = lax.rem(lon + lon_size - 2 * step, lon_size)
            for copy in kv_copies(row, owner, (lat, sibling), chips - 1 + step):
                copy.wait_recv()
                copy.start()

    def kv_collect(row):
        for step in range(chips):
            owner = lax.rem(sibling + lon_size - 2 * step, lon_size)
            for copy in kv_copies(row, owner, (lat, sibling), 0):
                copy.wait_recv()

    def mixed_copy(row):
        return pltpu.make_async_copy(mixed_field.at[row], mixed_out.at[row], out_sem.at[0, row])

    def attended_copy(row):
        return pltpu.make_async_copy(attended.at[row], attended_out.at[row], out_sem.at[1, row])

    def project(row):
        tokens = mixed_field[row].astype(jnp.float32)
        mean_square = jnp.mean(tokens * tokens, axis=-1, keepdims=True)
        scaled = tokens * lax.rsqrt(mean_square + 1e-06) * table_ref[GAIN_ROW]
        normed[row] = scaled.astype(jnp.bfloat16)
        both = jnp.dot(normed[row], key_value_weight[...], preferred_element_type=jnp.float32)
        keys[row, lon] = jnp.transpose(both[:, :BLOCK]).astype(jnp.bfloat16)
        values[row, lon] = both[:, BLOCK:].astype(jnp.bfloat16)
        kv_start(row)
        mixed_copy(row).start()

    def attend_row(row):
        kv_forward(row)
        place_queries(normed[row], query_weight, placed)
        kv_collect(row)

        def store(g, value):
            attended[row, :, g * BLOCK : (g + 1) * BLOCK] = value

        attend(placed, keys.at[row], values.at[row], mixed, store)
        attended_copy(row).start()

    positions = lax.broadcasted_iota(jnp.int32, circle_ref.shape, 0) + (lat * band - 2)
    angle = jnp.pi * (positions.astype(jnp.float32) + 0.5) / (band * lat_size)
    circle_ref[...] = jnp.abs(jnp.sin(angle))

    loads[0].wait()
    for side in sides:
        side.wait_recv()
    stencil(wide, 3, band - 2, 3, STENCIL_ONE_ROW, store_after_one, outward)
    loads[1].wait()
    loads[2].wait()

    def one_stage(stage, carry):
        @pl.when(stage < band)
        def _():
            @pl.when(at_pole)
            def _():
                @pl.when(stage == 0)
                def _():
                    halo_copy(0).wait_send()
                    halo_copy(1).wait_send()
                    halo_copy(3).start()

                @pl.when(stage == 1)
                def _():
                    halo_copy(2).start()

                @pl.when(stage > 1)
                def _():
                    halo_copy(stage).wait_send()

            @pl.when(jnp.logical_not(at_pole))
            def _():
                halo_copy(stage).wait_send()

                @pl.when(stage < band - 1)
                def _():
                    halo_copy(stage + 1).start()

            halo_arrival(stage).wait_recv()
            for edge in edges(stage):
                edge.start()
            for edge in edges(stage):
                edge.wait_recv()
            row = mixed_row(stage)
            outer = jnp.where(from_top(stage), row + 1, row + 3)
            stencil(wide, outer, 1, outer, STENCIL_ONE_ROW, store_after_one, outward)
            stencil(after_one, row + 1, 1, row + 2, STENCIL_TWO_ROW, store_mixed, inner)
            project(row)

        @pl.when(stage > 0)
        def _():
            attend_row(mixed_row(stage - 1))

        return carry

    lax.fori_loop(0, band + 1, one_stage, 0)

    for side in sides:
        side.wait_send()

    def finish(row, carry):
        for edge in edges(row):
            edge.wait_send()
        for slot in range(lon_size - 1):
            for copy in kv_copies(row, lon, (lat, sibling), slot):
                copy.wait_send()
        mixed_copy(row).wait()
        attended_copy(row).wait()
        return carry

    lax.fori_loop(0, band, finish, 0)


def local(grid_state, stencil_one, stencil_two, norm_gain, query_weight, key_value_weight):
    level_count, band, width, channels = grid_state.shape
    lat_size, lon_size = lax.axis_size("lat"), lax.axis_size("lon")
    table = jnp.stack(
        [stencil_one[a, b] for a in range(2) for b in range(3)]
        + [stencil_two[a, b] for a in range(2) for b in range(3)]
        + [norm_gain]
    )[:, None]
    whole = pl.BlockSpec(memory_space=pltpu.VMEM)
    anywhere = pl.BlockSpec(memory_space=pl.ANY)
    field = jax.ShapeDtypeStruct((band, width, channels), jnp.bfloat16)
    wide_width = width + 2 * EDGE
    rows = (band, width, channels)
    dma = pltpu.SemaphoreType.DMA
    mixed_field, attended = pl.pallas_call(
        functools.partial(block_kernel, lat_size, lon_size),
        out_shape=(field, field),
        in_specs=[
            whole,
            anywhere,
            anywhere,
            anywhere,
        ],
        out_specs=(anywhere, anywhere),
        scratch_shapes=[
            pltpu.VMEM((band + 4, wide_width, channels), jnp.bfloat16),
            pltpu.VMEM((band + 2, wide_width, channels), jnp.bfloat16),
            pltpu.VMEM(rows, jnp.bfloat16),
            pltpu.VMEM(rows, jnp.bfloat16),
            pltpu.VMEM((band, lon_size, BLOCK, width), jnp.bfloat16),
            pltpu.VMEM((band, lon_size, width, BLOCK), jnp.bfloat16),
            pltpu.VMEM((GROUPS, KV_HEADS, width, BLOCK), jnp.bfloat16),
            pltpu.VMEM((GROUPS, width, BLOCK), jnp.float32),
            pltpu.VMEM(rows, jnp.bfloat16),
            pltpu.VMEM(query_weight.shape, jnp.bfloat16),
            pltpu.VMEM(key_value_weight.shape, jnp.bfloat16),
            pltpu.VMEM((band + 4, 1, 128), jnp.float32),
            dma((3,)),
            dma((2, band)),
            dma((4,)),
            dma((4,)),
            dma((2,)),
            dma((2,)),
            dma((4, 2)),
            dma((4, 2)),
            dma((2, band, lon_size - 1)),
            dma((2, band, lon_size)),
        ],
        compiler_params=pltpu.CompilerParams(
            collective_id=0, has_side_effects=True, vmem_limit_bytes=56 * 1024 * 1024
        ),
    )(
        table,
        grid_state[0],
        query_weight,
        key_value_weight,
    )
    return (mixed_field[None], attended[None])


def solution(mesh):
    in_specs = (P(None, "lat", "lon", None), P(), P(), P(), P(), P())
    out_specs = (P(None, "lat", "lon", None), P(None, "lat", "lon", None))
    return jax.shard_map(local, mesh=mesh, in_specs=in_specs, out_specs=out_specs, check_vma=False)
```

```python
import functools
import math

import jax
import jax.numpy as jnp
from jax import lax
from jax.experimental import pallas as pl
from jax.experimental.pallas import tpu as pltpu
from jax.sharding import PartitionSpec as P

HEADS = 16
KV_HEADS = 4
HEAD_DIM = 64
GROUPS = HEADS // KV_HEADS
BLOCK = KV_HEADS * HEAD_DIM
EDGE = 16
MESH = pl.DeviceIdType.MESH
QUERY_SCALE = math.log2(math.e) / math.sqrt(HEAD_DIM)
BUNDLE = 2


def lane_group(shape):
    return lax.broadcasted_iota(jnp.int32, shape, len(shape) - 1) // HEAD_DIM


def place_queries(normed, query_weight_ref, placed_ref):
    for g in range(KV_HEADS):
        weight = query_weight_ref[:, g * BLOCK : (g + 1) * BLOCK]
        block = jnp.dot(normed, weight, preferred_element_type=jnp.float32) * QUERY_SCALE
        group = lane_group(block.shape)
        for j in range(GROUPS):
            shift = (g - j) * HEAD_DIM % BLOCK
            moved = pltpu.roll(block, shift, 1) if shift else block
            placed_ref[j, g] = jnp.where(group == g, moved, 0.0).astype(jnp.bfloat16)


def attend(placed_ref, keys_ref, values_ref, mixed_ref, store):
    owners = range(keys_ref.shape[0])
    columns = keys_ref.shape[0] * keys_ref.shape[2]
    width = mixed_ref.shape[1]
    bundles = [(j, g) for j in range(GROUPS) for g in range(0, KV_HEADS, BUNDLE)]

    def scores_of(bundle):
        j, g = bundle
        query = placed_ref[j, g : g + BUNDLE].reshape(BUNDLE * width, BLOCK)
        return [
            jnp.dot(query, keys_ref[o], preferred_element_type=jnp.float32) for o in owners
        ]

    scores = scores_of(bundles[0])
    for index, (j, first) in enumerate(bundles):
        following = scores_of(bundles[index + 1]) if index + 1 < len(bundles) else None
        peak = jnp.max(functools.reduce(jnp.maximum, scores), axis=-1, keepdims=True)
        probs = [jnp.exp2(part - peak) for part in scores]
        denominator = jnp.sum(sum(probs[1:], probs[0]), axis=-1, keepdims=True)
        rounded = jnp.concatenate([part.astype(jnp.bfloat16) for part in probs], axis=1)
        update = jnp.dot(
            rounded, values_ref[...].reshape(columns, BLOCK), preferred_element_type=jnp.float32
        ) * (1.0 / denominator)
        for g in range(first, first + BUNDLE):
            part = update[(g - first) * width : (g - first + 1) * width]
            mixed = part if g == 0 else jnp.where(lane_group(part.shape) == g, part, mixed)
        if first + BUNDLE == KV_HEADS:
            mixed_ref[j] = mixed
        scores = following
    for g in range(KV_HEADS):
        out = jnp.zeros(mixed_ref.shape[1:], jnp.float32)
        group = lane_group(out.shape)
        for j in range(GROUPS):
            shift = (j - g) * HEAD_DIM % BLOCK
            part = mixed_ref[j]
            moved = pltpu.roll(part, shift, 1) if shift else part
            out = jnp.where(group == j, moved, out)
        store(g, out.astype(jnp.bfloat16))


def block_kernel(
    lat_size,
    lon_size,
    *refs,
):
    taps_one, taps_two, gain_ref = refs[:6], refs[6:12], refs[12]
    (
    grid_ref,
    query_hbm,
    key_value_hbm,
    mixed_out,
    attended_out,
    wide,
    after_one,
    mixed_field,
    normed,
    keys,
    values,
    placed,
    mixed,
    attended,
    query_weight,
    key_value_weight,
    circle_ref,
    local_sem,
    out_sem,
    halo_send,
    halo_recv,
    side_send,
    side_recv,
    edge_send,
    edge_recv,
    kv_send,
    kv_recv,
    ) = refs[13:]
    band, width, channels = grid_ref.shape
    last = band - 1
    lat = lax.axis_index("lat")
    lon = lax.axis_index("lon")
    chips = lon_size // 2
    left, right = lax.rem(lon + lon_size - 1, lon_size), lax.rem(lon + 1, lon_size)
    sibling = lon + 1 - 2 * lax.rem(lon, 2)
    partner = lax.rem(lon + lon_size // 2, lon_size)
    top = (jnp.where(lat == 0, lat, lat - 1), jnp.where(lat == 0, partner, lon))
    at_end = lat == lat_size - 1
    bottom = (jnp.where(at_end, lat, lat + 1), jnp.where(at_end, partner, lon))

    def remote(src, dst, send, recv, device):
        return pltpu.make_async_remote_copy(
            src_ref=src,
            dst_ref=dst,
            send_sem=send,
            recv_sem=recv,
            device_id=device,
            device_id_type=MESH,
        )

    loads = [
        pltpu.make_async_copy(
            grid_ref, wide.at[pl.ds(2, band), pl.ds(EDGE, width)], local_sem.at[0]
        ),
        pltpu.make_async_copy(key_value_hbm, key_value_weight, local_sem.at[1]),
        pltpu.make_async_copy(query_hbm, query_weight, local_sem.at[2]),
    ]
    for load in loads:
        load.start()

    barrier = pltpu.get_barrier_semaphore()
    for device in (top, bottom):
        pl.semaphore_signal(barrier, inc=1, device_id=device, device_id_type=MESH)
    for step in range(1, lon_size):
        other = (lat, lax.rem(lon + step, lon_size))
        pl.semaphore_signal(barrier, inc=1, device_id=other, device_id_type=MESH)
    pl.semaphore_wait(barrier, lon_size + 1)

    def from_top(stage):
        return lax.rem(lat + stage, 2) == 1

    def halo_row(stage):
        far = stage // 2
        return jnp.where(from_top(stage), 1 - far, band + 2 + far)

    def mixed_row(stage):
        near = 1 - stage // 2
        return jnp.where(from_top(stage), near, last - near)

    def halo_copy(stage):
        far = stage // 2
        up = from_top(stage)
        pole = lat == jnp.where(up, 0, lat_size - 1)
        source = jnp.where(up, far, last - far)
        target = jnp.where(up == pole, 1 - far, band + 2 + far)
        device = (
            jnp.where(pole, lat, jnp.where(up, lat - 1, lat + 1)),
            jnp.where(pole, partner, lon),
        )
        return remote(
            grid_ref.at[source],
            wide.at[target, pl.ds(EDGE, width)],
            halo_send.at[stage],
            halo_recv.at[stage],
            device,
        )

    def halo_arrival(stage):
        block = wide.at[halo_row(stage), pl.ds(EDGE, width)]
        return remote(block, block, halo_send.at[stage], halo_recv.at[stage], (lat, sibling))

    sides = [
        remote(
            grid_ref.at[:, pl.ds(width - EDGE, EDGE)],
            wide.at[pl.ds(2, band), pl.ds(0, EDGE)],
            side_send.at[0],
            side_recv.at[0],
            (lat, right),
        ),
        remote(
            grid_ref.at[:, pl.ds(0, EDGE)],
            wide.at[pl.ds(2, band), pl.ds(EDGE + width, EDGE)],
            side_send.at[1],
            side_recv.at[1],
            (lat, left),
        ),
    ]
    for side in sides:
        side.start()
    halo_copy(0).start()

    at_pole = jnp.logical_or(lat == 0, at_end)

    @pl.when(at_pole)
    def _():
        halo_copy(1).start()

    def edges(stage):
        row = halo_row(stage)
        return [
            remote(
                wide.at[row, pl.ds(width, EDGE)],
                wide.at[row, pl.ds(0, EDGE)],
                edge_send.at[stage, 0],
                edge_recv.at[stage, 0],
                (lat, right),
            ),
            remote(
                wide.at[row, pl.ds(EDGE, EDGE)],
                wide.at[row, pl.ds(EDGE + width, EDGE)],
                edge_send.at[stage, 1],
                edge_recv.at[stage, 1],
                (lat, left),
            ),
        ]

    def stencil(source, first, count, circle_first, weights, store, strips):
        chunks = channels // 128

        def one(index, carry):
            row = first + index // chunks
            circle = circle_first + index // chunks
            lanes = pl.ds(pl.multiple_of(index % chunks * 128, 128), 128)
            factors = [circle_ref[circle + offset] for offset in (-1, 0, 1)]
            own = [weights[offset][:, lanes] * factors[1] for offset in range(3)]
            next_to = [weights[3 + offset][:, lanes] for offset in range(3)]

            def taps(strip):
                columns = pl.ds(strip * EDGE, EDGE)
                above = source[row - 1, columns, lanes].astype(jnp.float32)
                centre = source[row, columns, lanes].astype(jnp.float32)
                below = source[row + 1, columns, lanes].astype(jnp.float32)
                beside = factors[0] * above + factors[2] * below
                parts = [own[offset] * centre + next_to[offset] * beside for offset in range(3)]
                return parts[0], centre + parts[1], parts[2]

            start, stop = strips
            before, here = taps(max(start - 1, 0)), taps(start)
            for strip in range(start, stop):
                after = taps(min(strip + 1, width // EDGE + 1))
                west = jnp.concatenate([before[0][8:], here[0]], axis=0)
                east = jnp.concatenate([here[2], after[2][:8]], axis=0)
                result = here[1] + pltpu.roll(west, 1, 0)[8:] + pltpu.roll(east, 23, 0)[:EDGE]
                store(row, strip, lanes, result.astype(jnp.bfloat16))
                before, here = here, after
            return carry

        lax.fori_loop(0, count * chunks, one, 0)

    inner = (1, width // EDGE + 1)
    outward = (0, width // EDGE + 2)

    def store_after_one(row, strip, lanes, value):
        after_one[row - 1, pl.ds(strip * EDGE, EDGE), lanes] = value

    def store_mixed(row, strip, lanes, value):
        mixed_field[row - 1, pl.ds((strip - 1) * EDGE, EDGE), lanes] = value

    def kv_copies(row, owner, device, slot):
        return [
            remote(
                held.at[row, owner],
                held.at[row, owner],
                kv_send.at[kind, row, slot],
                kv_recv.at[kind, row, owner],
                device,
            )
            for kind, held in enumerate((keys, values))
        ]

    def kv_start(row):
        for step in range(1, chips):
            for copy in kv_copies(row, lon, (lat, lax.rem(lon + 2 * step, lon_size)), step):
                copy.start()
        for copy in kv_copies(row, lon, (lat, sibling), 0):
            copy.start()

    def kv_forward(row):
        for step in range(1, chips):
            owner = lax.rem(lon + lon_size - 2 * step, lon_size)
            for copy in kv_copies(row, owner, (lat, sibling), chips - 1 + step):
                copy.wait_recv()
                copy.start()

    def kv_collect(row):
        for step in range(chips):
            owner = lax.rem(sibling + lon_size - 2 * step, lon_size)
            for copy in kv_copies(row, owner, (lat, sibling), 0):
                copy.wait_recv()

    def mixed_copy(row):
        return pltpu.make_async_copy(mixed_field.at[row], mixed_out.at[row], out_sem.at[0, row])

    def attended_copy(row):
        return pltpu.make_async_copy(attended.at[row], attended_out.at[row], out_sem.at[1, row])

    def project(row):
        tokens = mixed_field[row].astype(jnp.float32)
        mean_square = jnp.mean(tokens * tokens, axis=-1, keepdims=True)
        scaled = tokens * lax.rsqrt(mean_square + 1e-06) * gain_ref[...]
        normed[row] = scaled.astype(jnp.bfloat16)
        both = jnp.dot(normed[row], key_value_weight[...], preferred_element_type=jnp.float32)
        keys[row, lon] = jnp.transpose(both[:, :BLOCK]).astype(jnp.bfloat16)
        values[row, lon] = both[:, BLOCK:].astype(jnp.bfloat16)
        kv_start(row)
        mixed_copy(row).start()

    def attend_row(row):
        kv_forward(row)
        place_queries(normed[row], query_weight, placed)
        kv_collect(row)

        def store(g, value):
            attended[row, :, g * BLOCK : (g + 1) * BLOCK] = value

        attend(placed, keys.at[row], values.at[row], mixed, store)
        attended_copy(row).start()

    positions = lax.broadcasted_iota(jnp.int32, circle_ref.shape, 0) + (lat * band - 2)
    angle = jnp.pi * (positions.astype(jnp.float32) + 0.5) / (band * lat_size)
    circle_ref[...] = jnp.abs(jnp.sin(angle))

    loads[0].wait()
    for side in sides:
        side.wait_recv()
    stencil(wide, 3, band - 2, 3, taps_one, store_after_one, outward)
    loads[1].wait()
    loads[2].wait()

    def one_half(half, carry):
        def one_stage(stage, carry):
            @pl.when(at_pole)
            def _():
                @pl.when(stage == 0)
                def _():
                    halo_copy(0).wait_send()
                    halo_copy(1).wait_send()
                    halo_copy(3).start()

                @pl.when(stage == 1)
                def _():
                    halo_copy(2).start()

                @pl.when(stage > 1)
                def _():
                    halo_copy(stage).wait_send()

            @pl.when(jnp.logical_not(at_pole))
            def _():
                halo_copy(stage).wait_send()

                @pl.when(stage == 0)
                def _():
                    halo_copy(1).start()

                @pl.when(stage == 1)
                def _():
                    halo_copy(2).start()
                    halo_copy(3).start()

            halo_arrival(stage).wait_recv()
            for edge in edges(stage):
                edge.start()
            for edge in edges(stage):
                edge.wait_recv()
            row = mixed_row(stage)
            outer = jnp.where(from_top(stage), row + 1, row + 3)
            stencil(wide, outer, 1, outer, taps_one, store_after_one, outward)
            stencil(after_one, row + 1, 1, row + 2, taps_two, store_mixed, inner)
            project(row)
            return carry

        def one_row(stage, carry):
            attend_row(mixed_row(stage))
            return carry

        lax.fori_loop(2 * half, 2 * half + 2, one_stage, 0)
        lax.fori_loop(2 * half, 2 * half + 2, one_row, 0)
        return carry

    lax.fori_loop(0, band // 2, one_half, 0)

    for side in sides:
        side.wait_send()

    def finish(row, carry):
        for edge in edges(row):
            edge.wait_send()
        for slot in range(lon_size - 1):
            for copy in kv_copies(row, lon, (lat, sibling), slot):
                copy.wait_send()
        mixed_copy(row).wait()
        attended_copy(row).wait()
        return carry

    lax.fori_loop(0, band, finish, 0)


def local(grid_state, stencil_one, stencil_two, norm_gain, query_weight, key_value_weight):
    level_count, band, width, channels = grid_state.shape
    lat_size, lon_size = lax.axis_size("lat"), lax.axis_size("lon")
    taps = [
        weights[beside, offset][None]
        for weights in (stencil_one, stencil_two)
        for beside in range(2)
        for offset in range(3)
    ]
    whole = pl.BlockSpec(memory_space=pltpu.VMEM)
    anywhere = pl.BlockSpec(memory_space=pl.ANY)
    field = jax.ShapeDtypeStruct((band, width, channels), jnp.bfloat16)
    wide_width = width + 2 * EDGE
    rows = (band, width, channels)
    dma = pltpu.SemaphoreType.DMA
    mixed_field, attended = pl.pallas_call(
        functools.partial(block_kernel, lat_size, lon_size),
        out_shape=(field, field),
        in_specs=[
            *[whole] * 13,
            anywhere,
            anywhere,
            anywhere,
        ],
        out_specs=(anywhere, anywhere),
        scratch_shapes=[
            pltpu.VMEM((band + 4, wide_width, channels), jnp.bfloat16),
            pltpu.VMEM((band + 2, wide_width, channels), jnp.bfloat16),
            pltpu.VMEM(rows, jnp.bfloat16),
            pltpu.VMEM(rows, jnp.bfloat16),
            pltpu.VMEM((band, lon_size, BLOCK, width), jnp.bfloat16),
            pltpu.VMEM((band, lon_size, width, BLOCK), jnp.bfloat16),
            pltpu.VMEM((GROUPS, KV_HEADS, width, BLOCK), jnp.bfloat16),
            pltpu.VMEM((GROUPS, width, BLOCK), jnp.float32),
            pltpu.VMEM(rows, jnp.bfloat16),
            pltpu.VMEM(query_weight.shape, jnp.bfloat16),
            pltpu.VMEM(key_value_weight.shape, jnp.bfloat16),
            pltpu.VMEM((band + 4, 1, 128), jnp.float32),
            dma((3,)),
            dma((2, band)),
            dma((4,)),
            dma((4,)),
            dma((2,)),
            dma((2,)),
            dma((4, 2)),
            dma((4, 2)),
            dma((2, band, lon_size - 1)),
            dma((2, band, lon_size)),
        ],
        compiler_params=pltpu.CompilerParams(
            collective_id=0, has_side_effects=True, vmem_limit_bytes=56 * 1024 * 1024
        ),
    )(
        *taps,
        norm_gain[None],
        grid_state[0],
        query_weight,
        key_value_weight,
    )
    return (mixed_field[None], attended[None])


def solution(mesh):
    in_specs = (P(None, "lat", "lon", None), P(), P(), P(), P(), P())
    out_specs = (P(None, "lat", "lon", None), P(None, "lat", "lon", None))
    return jax.shard_map(local, mesh=mesh, in_specs=in_specs, out_specs=out_specs, check_vma=False)
```

```python
import functools
import math

import jax
import jax.numpy as jnp
from jax import lax
from jax.experimental import pallas as pl
from jax.experimental.pallas import tpu as pltpu
from jax.sharding import PartitionSpec as P

HEADS = 16
KV_HEADS = 4
HEAD_DIM = 64
GROUPS = HEADS // KV_HEADS
BLOCK = KV_HEADS * HEAD_DIM
EDGE = 16
MESH = pl.DeviceIdType.MESH
QUERY_SCALE = math.log2(math.e) / math.sqrt(HEAD_DIM)
BUNDLE = 2


def lane_group(shape):
    return lax.broadcasted_iota(jnp.int32, shape, len(shape) - 1) // HEAD_DIM


def place_queries(normed, query_weight_ref, placed_ref):
    for g in range(KV_HEADS):
        weight = query_weight_ref[:, g * BLOCK : (g + 1) * BLOCK]
        block = jnp.dot(normed, weight, preferred_element_type=jnp.float32) * QUERY_SCALE
        group = lane_group(block.shape)
        for j in range(GROUPS):
            shift = (g - j) * HEAD_DIM % BLOCK
            moved = pltpu.roll(block, shift, 1) if shift else block
            placed_ref[j, g] = jnp.where(group == g, moved, 0.0).astype(jnp.bfloat16)


def attend(placed_ref, keys_ref, values_ref, mixed_ref, store, interlude):
    owners = range(keys_ref.shape[0])
    columns = keys_ref.shape[0] * keys_ref.shape[2]
    width = mixed_ref.shape[1]
    bundles = [(j, g) for j in range(GROUPS) for g in range(0, KV_HEADS, BUNDLE)]

    def scores_of(bundle):
        j, g = bundle
        query = placed_ref[j, g : g + BUNDLE].reshape(BUNDLE * width, BLOCK)
        return [
            jnp.dot(query, keys_ref[o], preferred_element_type=jnp.float32) for o in owners
        ]

    scores = scores_of(bundles[0])
    for index, (j, first) in enumerate(bundles):
        following = scores_of(bundles[index + 1]) if index + 1 < len(bundles) else None
        peak = jnp.max(functools.reduce(jnp.maximum, scores), axis=-1, keepdims=True)
        probs = [jnp.exp2(part - peak) for part in scores]
        denominator = jnp.sum(sum(probs[1:], probs[0]), axis=-1, keepdims=True)
        rounded = jnp.concatenate([part.astype(jnp.bfloat16) for part in probs], axis=1)
        update = jnp.dot(
            rounded, values_ref[...].reshape(columns, BLOCK), preferred_element_type=jnp.float32
        ) * (1.0 / denominator)
        for g in range(first, first + BUNDLE):
            part = update[(g - first) * width : (g - first + 1) * width]
            mixed = part if g == 0 else jnp.where(lane_group(part.shape) == g, part, mixed)
        if first + BUNDLE == KV_HEADS:
            mixed_ref[j] = mixed
        scores = following
        if index == 3 * len(bundles) // 4:
            interlude()
    for g in range(KV_HEADS):
        out = jnp.zeros(mixed_ref.shape[1:], jnp.float32)
        group = lane_group(out.shape)
        for j in range(GROUPS):
            shift = (j - g) * HEAD_DIM % BLOCK
            part = mixed_ref[j]
            moved = pltpu.roll(part, shift, 1) if shift else part
            out = jnp.where(group == j, moved, out)
        store(g, out.astype(jnp.bfloat16))


def block_kernel(
    lat_size,
    lon_size,
    *refs,
):
    taps_one, taps_two, gain_ref = refs[:6], refs[6:12], refs[12]
    (
    grid_ref,
    query_hbm,
    key_value_hbm,
    mixed_out,
    attended_out,
    wide,
    after_one,
    mixed_field,
    normed,
    keys,
    values,
    placed,
    mixed,
    attended,
    query_weight,
    key_value_weight,
    circle_ref,
    local_sem,
    out_sem,
    halo_send,
    halo_recv,
    side_send,
    side_recv,
    edge_send,
    edge_recv,
    kv_send,
    kv_recv,
    ) = refs[13:]
    band, width, channels = grid_ref.shape
    last = band - 1
    lat = lax.axis_index("lat")
    lon = lax.axis_index("lon")
    chips = lon_size // 2
    left, right = lax.rem(lon + lon_size - 1, lon_size), lax.rem(lon + 1, lon_size)
    sibling = lon + 1 - 2 * lax.rem(lon, 2)
    partner = lax.rem(lon + lon_size // 2, lon_size)
    top = (jnp.where(lat == 0, lat, lat - 1), jnp.where(lat == 0, partner, lon))
    at_end = lat == lat_size - 1
    bottom = (jnp.where(at_end, lat, lat + 1), jnp.where(at_end, partner, lon))

    def remote(src, dst, send, recv, device):
        return pltpu.make_async_remote_copy(
            src_ref=src,
            dst_ref=dst,
            send_sem=send,
            recv_sem=recv,
            device_id=device,
            device_id_type=MESH,
        )

    loads = [
        pltpu.make_async_copy(
            grid_ref, wide.at[pl.ds(2, band), pl.ds(EDGE, width)], local_sem.at[0]
        ),
        pltpu.make_async_copy(key_value_hbm, key_value_weight, local_sem.at[1]),
        pltpu.make_async_copy(query_hbm, query_weight, local_sem.at[2]),
    ]
    for load in loads:
        load.start()

    barrier = pltpu.get_barrier_semaphore()
    for device in (top, bottom):
        pl.semaphore_signal(barrier, inc=1, device_id=device, device_id_type=MESH)
    for step in range(1, lon_size):
        other = (lat, lax.rem(lon + step, lon_size))
        pl.semaphore_signal(barrier, inc=1, device_id=other, device_id_type=MESH)
    pl.semaphore_wait(barrier, lon_size + 1)

    def from_top(stage):
        return lax.rem(lat + stage, 2) == 1

    def halo_row(stage):
        far = stage // 2
        return jnp.where(from_top(stage), 1 - far, band + 2 + far)

    def mixed_row(stage):
        near = 1 - stage // 2
        return jnp.where(from_top(stage), near, last - near)

    def halo_copy(stage):
        far = stage // 2
        up = from_top(stage)
        pole = lat == jnp.where(up, 0, lat_size - 1)
        source = jnp.where(up, far, last - far)
        target = jnp.where(up == pole, 1 - far, band + 2 + far)
        device = (
            jnp.where(pole, lat, jnp.where(up, lat - 1, lat + 1)),
            jnp.where(pole, partner, lon),
        )
        return remote(
            grid_ref.at[source],
            wide.at[target, pl.ds(EDGE, width)],
            halo_send.at[stage],
            halo_recv.at[stage],
            device,
        )

    def halo_arrival(stage):
        block = wide.at[halo_row(stage), pl.ds(EDGE, width)]
        return remote(block, block, halo_send.at[stage], halo_recv.at[stage], (lat, sibling))

    sides = [
        remote(
            grid_ref.at[:, pl.ds(width - EDGE, EDGE)],
            wide.at[pl.ds(2, band), pl.ds(0, EDGE)],
            side_send.at[0],
            side_recv.at[0],
            (lat, right),
        ),
        remote(
            grid_ref.at[:, pl.ds(0, EDGE)],
            wide.at[pl.ds(2, band), pl.ds(EDGE + width, EDGE)],
            side_send.at[1],
            side_recv.at[1],
            (lat, left),
        ),
    ]
    for side in sides:
        side.start()
    halo_copy(0).start()

    at_pole = jnp.logical_or(lat == 0, at_end)

    @pl.when(at_pole)
    def _():
        halo_copy(1).start()

    def edges(stage):
        row = halo_row(stage)
        return [
            remote(
                wide.at[row, pl.ds(width, EDGE)],
                wide.at[row, pl.ds(0, EDGE)],
                edge_send.at[stage, 0],
                edge_recv.at[stage, 0],
                (lat, right),
            ),
            remote(
                wide.at[row, pl.ds(EDGE, EDGE)],
                wide.at[row, pl.ds(EDGE + width, EDGE)],
                edge_send.at[stage, 1],
                edge_recv.at[stage, 1],
                (lat, left),
            ),
        ]

    def stencil(source, first, count, circle_first, weights, store, strips):
        chunks = channels // 128

        def one(index, carry):
            row = first + index // chunks
            circle = circle_first + index // chunks
            lanes = pl.ds(pl.multiple_of(index % chunks * 128, 128), 128)
            factors = [circle_ref[circle + offset] for offset in (-1, 0, 1)]
            own = [weights[offset][:, lanes] * factors[1] for offset in range(3)]
            next_to = [weights[3 + offset][:, lanes] for offset in range(3)]

            def taps(strip):
                columns = pl.ds(strip * EDGE, EDGE)
                above = source[row - 1, columns, lanes].astype(jnp.float32)
                centre = source[row, columns, lanes].astype(jnp.float32)
                below = source[row + 1, columns, lanes].astype(jnp.float32)
                beside = factors[0] * above + factors[2] * below
                parts = [own[offset] * centre + next_to[offset] * beside for offset in range(3)]
                return parts[0], centre + parts[1], parts[2]

            start, stop = strips
            before, here = taps(max(start - 1, 0)), taps(start)
            for strip in range(start, stop):
                after = taps(min(strip + 1, width // EDGE + 1))
                west = jnp.concatenate([before[0][8:], here[0]], axis=0)
                east = jnp.concatenate([here[2], after[2][:8]], axis=0)
                result = here[1] + pltpu.roll(west, 1, 0)[8:] + pltpu.roll(east, 23, 0)[:EDGE]
                store(row, strip, lanes, result.astype(jnp.bfloat16))
                before, here = here, after
            return carry

        lax.fori_loop(0, count * chunks, one, 0)

    inner = (1, width // EDGE + 1)
    outward = (0, width // EDGE + 2)

    def store_after_one(row, strip, lanes, value):
        after_one[row - 1, pl.ds(strip * EDGE, EDGE), lanes] = value

    def store_mixed(row, strip, lanes, value):
        mixed_field[row - 1, pl.ds((strip - 1) * EDGE, EDGE), lanes] = value

    def kv_copies(row, owner, device, slot):
        return [
            remote(
                held.at[row, owner],
                held.at[row, owner],
                kv_send.at[kind, row, slot],
                kv_recv.at[kind, row, owner],
                device,
            )
            for kind, held in enumerate((keys, values))
        ]

    def kv_start(row):
        for step in range(1, chips):
            for copy in kv_copies(row, lon, (lat, lax.rem(lon + 2 * step, lon_size)), step):
                copy.start()
        for copy in kv_copies(row, lon, (lat, sibling), 0):
            copy.start()

    def kv_forward(row):
        for step in range(1, chips):
            owner = lax.rem(lon + lon_size - 2 * step, lon_size)
            for copy in kv_copies(row, owner, (lat, sibling), chips - 1 + step):
                copy.wait_recv()
                copy.start()

    def kv_collect(row):
        for step in range(chips):
            owner = lax.rem(sibling + lon_size - 2 * step, lon_size)
            for copy in kv_copies(row, owner, (lat, sibling), 0):
                copy.wait_recv()

    def mixed_copy(row):
        return pltpu.make_async_copy(mixed_field.at[row], mixed_out.at[row], out_sem.at[0, row])

    def attended_copy(row):
        return pltpu.make_async_copy(attended.at[row], attended_out.at[row], out_sem.at[1, row])

    def project(row):
        tokens = mixed_field[row].astype(jnp.float32)
        mean_square = jnp.mean(tokens * tokens, axis=-1, keepdims=True)
        scaled = tokens * lax.rsqrt(mean_square + 1e-06) * gain_ref[...]
        normed[row] = scaled.astype(jnp.bfloat16)
        both = jnp.dot(normed[row], key_value_weight[...], preferred_element_type=jnp.float32)
        keys[row, lon] = jnp.transpose(both[:, :BLOCK]).astype(jnp.bfloat16)
        values[row, lon] = both[:, BLOCK:].astype(jnp.bfloat16)
        kv_start(row)
        mixed_copy(row).start()

    def attend_row(row, interlude):
        kv_forward(row)
        place_queries(normed[row], query_weight, placed)
        kv_collect(row)

        def store(g, value):
            attended[row, :, g * BLOCK : (g + 1) * BLOCK] = value

        attend(placed, keys.at[row], values.at[row], mixed, store, interlude)
        attended_copy(row).start()

    positions = lax.broadcasted_iota(jnp.int32, circle_ref.shape, 0) + (lat * band - 2)
    angle = jnp.pi * (positions.astype(jnp.float32) + 0.5) / (band * lat_size)
    circle_ref[...] = jnp.abs(jnp.sin(angle))

    loads[0].wait()
    for side in sides:
        side.wait_recv()
    stencil(wide, 3, band - 2, 3, taps_one, store_after_one, outward)
    loads[1].wait()
    loads[2].wait()

    def one_stage(stage, carry):
        @pl.when(stage < band)
        def _():
            @pl.when(at_pole)
            def _():
                @pl.when(stage == 0)
                def _():
                    halo_copy(0).wait_send()
                    halo_copy(1).wait_send()
                    halo_copy(3).start()

                @pl.when(stage == 1)
                def _():
                    halo_copy(2).start()

                @pl.when(stage > 1)
                def _():
                    halo_copy(stage).wait_send()

            @pl.when(jnp.logical_and(stage != 2, jnp.logical_not(at_pole)))
            def _():
                halo_copy(stage).wait_send()

                @pl.when(stage < 2)
                def _():
                    halo_copy(stage + 1).start()

            halo_arrival(stage).wait_recv()
            for edge in edges(stage):
                edge.start()
            for edge in edges(stage):
                edge.wait_recv()
            row = mixed_row(stage)
            outer = jnp.where(from_top(stage), row + 1, row + 3)
            stencil(wide, outer, 1, outer, taps_one, store_after_one, outward)
            stencil(after_one, row + 1, 1, row + 2, taps_two, store_mixed, inner)
            project(row)

        @pl.when(stage > 0)
        def _():
            def interlude():
                @pl.when(jnp.logical_and(stage == 1, jnp.logical_not(at_pole)))
                def _():
                    halo_copy(2).wait_send()
                    halo_copy(3).start()

            attend_row(mixed_row(stage - 1), interlude)

        return carry

    lax.fori_loop(0, band + 1, one_stage, 0)

    for side in sides:
        side.wait_send()

    def finish(row, carry):
        for edge in edges(row):
            edge.wait_send()
        for slot in range(lon_size - 1):
            for copy in kv_copies(row, lon, (lat, sibling), slot):
                copy.wait_send()
        mixed_copy(row).wait()
        attended_copy(row).wait()
        return carry

    lax.fori_loop(0, band, finish, 0)


def local(grid_state, stencil_one, stencil_two, norm_gain, query_weight, key_value_weight):
    level_count, band, width, channels = grid_state.shape
    lat_size, lon_size = lax.axis_size("lat"), lax.axis_size("lon")
    taps = [
        weights[beside, offset][None]
        for weights in (stencil_one, stencil_two)
        for beside in range(2)
        for offset in range(3)
    ]
    whole = pl.BlockSpec(memory_space=pltpu.VMEM)
    anywhere = pl.BlockSpec(memory_space=pl.ANY)
    field = jax.ShapeDtypeStruct((band, width, channels), jnp.bfloat16)
    wide_width = width + 2 * EDGE
    rows = (band, width, channels)
    dma = pltpu.SemaphoreType.DMA
    mixed_field, attended = pl.pallas_call(
        functools.partial(block_kernel, lat_size, lon_size),
        out_shape=(field, field),
        in_specs=[
            *[whole] * 13,
            anywhere,
            anywhere,
            anywhere,
        ],
        out_specs=(anywhere, anywhere),
        scratch_shapes=[
            pltpu.VMEM((band + 4, wide_width, channels), jnp.bfloat16),
            pltpu.VMEM((band + 2, wide_width, channels), jnp.bfloat16),
            pltpu.VMEM(rows, jnp.bfloat16),
            pltpu.VMEM(rows, jnp.bfloat16),
            pltpu.VMEM((band, lon_size, BLOCK, width), jnp.bfloat16),
            pltpu.VMEM((band, lon_size, width, BLOCK), jnp.bfloat16),
            pltpu.VMEM((GROUPS, KV_HEADS, width, BLOCK), jnp.bfloat16),
            pltpu.VMEM((GROUPS, width, BLOCK), jnp.float32),
            pltpu.VMEM(rows, jnp.bfloat16),
            pltpu.VMEM(query_weight.shape, jnp.bfloat16),
            pltpu.VMEM(key_value_weight.shape, jnp.bfloat16),
            pltpu.VMEM((band + 4, 1, 128), jnp.float32),
            dma((3,)),
            dma((2, band)),
            dma((4,)),
            dma((4,)),
            dma((2,)),
            dma((2,)),
            dma((4, 2)),
            dma((4, 2)),
            dma((2, band, lon_size - 1)),
            dma((2, band, lon_size)),
        ],
        compiler_params=pltpu.CompilerParams(
            collective_id=0, has_side_effects=True, vmem_limit_bytes=56 * 1024 * 1024
        ),
    )(
        *taps,
        norm_gain[None],
        grid_state[0],
        query_weight,
        key_value_weight,
    )
    return (mixed_field[None], attended[None])


def solution(mesh):
    in_specs = (P(None, "lat", "lon", None), P(), P(), P(), P(), P())
    out_specs = (P(None, "lat", "lon", None), P(None, "lat", "lon", None))
    return jax.shard_map(local, mesh=mesh, in_specs=in_specs, out_specs=out_specs, check_vma=False)
```
